128 devices in a mesh: dp: 64 (over x_lo, y, z, core), expert: 2 (over x_hi).
Axes of the slice: x: 4 (x_hi: 2, x_lo: 2; x = x_hi * 2 + x_lo), y: 4, z: 4, core: 2. Of those that a mesh axis runs over, the one named last changes fastest.
Arguments:
- tokens: bfloat16 [131072, 3584], P(('dp', 'expert')), may hold values from -6 to 6
- assignment: int32 [131072, 1], P(('dp', 'expert')), may hold values from 0 to 1; in each aligned block of 1024 rows (0 to 1023, 1024 to 2047, ...) at most 640 rows name the same one
- gate: bfloat16 [131072], P(('dp', 'expert')), may hold values from 0.099609375 to 1
- weight: bfloat16 [2, 3584, 1024], P('expert', 'dp'), may hold values from -0.09375 to 0.09375
- cotangent: bfloat16 [2, 81920, 1024], P('expert', 'dp'), may hold values from -6 to 6
Outputs:
- activated: bfloat16 [2, 81920, 1024], P('expert', 'dp')
- grad_tokens: bfloat16 [131072, 3584], P(('dp', 'expert'))
- grad_gate: bfloat16 [131072], P(('dp', 'expert'))
- grad_weight: float32 [2, 3584, 1024], P('expert', 'dp')
The draws below stay inside these ranges and needn't reach their ends.
Inputs may be any that keep to these rules, and one draw needn't show every extreme that they name: `assignment`: of the tokens of one device at most 640 name the same expert, and in some device exactly 640 do.
All inputs are finite; a program needn't handle non-finite values.
Results may differ from the reference program's by a relative error of at most 0.0049.
Values may be sent and summed in bfloat16 or wider, within the bound.
A program may use at most 128 MiB of HBM per device.

```python
import math
import jax
import jax.numpy as jnp
import numpy as np

D = 3584
F = 1024
TOK_DEV = 1024
CAP = 640
EXPERTS = 2
TOKENS = 131072
SLOTS = 81920
N_DP = 64
N_EXPERT = 2


def shard_levels(rng, extent, pieces, low, high):
    factor_of, own = 1.0, jax.random.fold_in(rng, 6)
    for dim, shards_of in pieces:
        heights = jnp.exp(jax.random.uniform(jax.random.fold_in(own, dim), (shards_of,), jnp.float32, low / len(pieces), high / len(pieces)))
        factor_of = factor_of * jnp.repeat(heights, extent[dim] // shards_of).reshape([-1 if axis == dim else 1 for axis in range(len(extent))])
    return factor_of


def deal_out(key, own, number, rows, number_of, top, bound, skew):
    order = jax.random.permutation(key, number_of)
    heavy_load, common = shares(number_of, rows * top, bound, skew, True), shares(number_of, rows * top, bound, skew, False)
    places = jnp.arange(number_of)

    def named(tallies, offset_by):
        used = int((tallies > 0).sum())
        fixed = max(1, used // 4)
        shifted = fixed + (places - fixed + offset_by * (used - fixed)) % max(1, number_of - fixed)
        return jnp.zeros((number_of,), jnp.int32).at[order[jnp.where(places < fixed, places, shifted)]].set(jnp.asarray(tallies, jnp.int32))

    tallies = jnp.where(number % 4 == 0, named(heavy_load, number // 4), named(common, number - number // 4 - 1))
    mixed = jax.random.permutation(jax.random.fold_in(own, 3), number_of)
    giver, taker = mixed[0:number_of // 2 * 2:2], mixed[1:number_of // 2 * 2:2]
    margin = jnp.minimum(tallies[giver] - 1, bound - tallies[taker]) // 2
    margin = jnp.where((giver == order[0]) | (taker == order[0]) | (tallies[taker] == 0), 0, jnp.maximum(margin, 0))
    shifted = jax.random.randint(jax.random.fold_in(own, 4), (number_of // 2,), 0, 1 << 20) % (margin + 1)
    tallies = tallies.at[giver].add(-shifted).at[taker].add(shifted)
    members = jnp.searchsorted(jnp.cumsum(tallies), jnp.arange(rows * top), side="right").astype(jnp.int32)
    table = members.reshape(top, rows).T
    table = table[jax.random.permutation(jax.random.fold_in(own, 1), rows)]
    offset_by = jax.random.randint(jax.random.fold_in(own, 2), (rows, 1), 0, top)
    return jnp.take_along_axis(table, (jnp.arange(top)[None, :] + offset_by) % top, axis=1)


def shares(amount, total, reach, lean, full):
    portions = [(1 << 20) // math.isqrt(standing ** lean) + 1 for standing in range(1, amount + 1)]
    largest = reach if full else min(reach, max(-(-total // amount), total * portions[0] // sum(portions)))
    least = 1 if total - largest >= amount - 1 else 0
    holding, spare = [largest] + [least] * (amount - 1), total - largest - least * (amount - 1)
    while spare > 0:
        movable = [i for i in range(1, amount) if holding[i] < largest] or [i for i in range(1, amount) if holding[i] < reach]
        pool, budget = sum([portions[i] for i in movable]), spare
        for i in movable:
            more = min(reach - holding[i], max(1, budget * portions[i] // pool), spare)
            holding[i] = holding[i] + more
            spare = spare - more
    return np.array(holding)


def centred(key, extent, spread, bound, split=(), kind=jnp.bfloat16):
    drawn = spread * jax.random.normal(key, extent, jnp.float32)
    if split:
        drawn = drawn * shard_levels(key, extent, split, -0.22, 0.18)
    return jnp.clip(drawn, -bound, bound).astype(kind)


def setup_inputs(seed: int = 0) -> dict:
    streams_of = jax.random.split(jax.random.key(seed), 6)
    tokens = centred(streams_of[0], (TOKENS, D), 1.0, 6.0, ((0, 128),))
    assignment_keys = jax.random.split(jax.random.fold_in(streams_of[1], 1), TOKENS // TOK_DEV)
    assignment_turns = jax.random.permutation(jax.random.fold_in(streams_of[1], 3), TOKENS // TOK_DEV)
    assignment = jax.vmap(lambda own, number: deal_out(jax.random.fold_in(streams_of[1], 2), own, number, TOK_DEV, EXPERTS, 1, CAP, 2))(assignment_keys, assignment_turns).reshape((TOKENS, 1))
    gate = jnp.clip(jnp.exp(math.log(1.0) - 2.306499 * jax.random.uniform(streams_of[2], (TOKENS,), jnp.float32) ** shard_levels(streams_of[2], (TOKENS,), ((0, 128),), -0.2, 0.2)), 0.099609375, 1.0).astype(jnp.bfloat16)
    weight = centred(streams_of[3], (EXPERTS, D, F), D ** -0.5, 0.09375, ((0, 2), (1, 64)))
    cotangent = centred(streams_of[4], (EXPERTS, SLOTS, F), 1.0, 6.0, ((0, 2), (1, 64)))
    return dict(tokens=tokens, assignment=assignment, gate=gate, weight=weight, cotangent=cotangent)


def reference(tokens, assignment, gate, weight, cotangent):
    blocks = N_DP * N_EXPERT
    owner = assignment[:, 0]
    local_owner = owner.reshape(blocks, TOK_DEV)
    onehot = (local_owner[:, :, None] == jnp.arange(EXPERTS, dtype=jnp.int32)[None, None, :]).astype(jnp.int32)
    ranks = jnp.sum((jnp.cumsum(onehot, axis=1) - 1) * onehot, axis=2)
    block_ids = jnp.arange(blocks, dtype=jnp.int32)[:, None]
    rows = (block_ids * CAP + ranks).reshape(-1).astype(jnp.int32)
    grad_tokens = jnp.zeros((TOKENS, D), jnp.bfloat16)
    grad_gate = jnp.zeros((TOKENS,), jnp.bfloat16)
    activated_list = []
    weight_list = []
    for expert in range(EXPERTS):
        chosen = owner == expert
        places = jnp.where(chosen, rows, SLOTS).astype(jnp.int32)
        slot_rows = jnp.zeros((SLOTS, D), jnp.bfloat16).at[places].set(tokens, mode="drop")
        slot_gate = jnp.zeros((SLOTS,), jnp.bfloat16).at[places].set(gate, mode="drop")
        gate_values = slot_gate.astype(jnp.float32)[:, None]
        preact = jnp.dot(slot_rows, weight[expert], preferred_element_type=jnp.float32)
        sigma = jax.nn.sigmoid(preact)
        shaped = preact * sigma
        activated_list.append((gate_values * shaped).astype(jnp.bfloat16))
        upstream = cotangent[expert].astype(jnp.float32)
        slot_gate_grad = jnp.sum(upstream * shaped, axis=1).astype(jnp.bfloat16)
        slope = sigma * (1.0 + preact * (1.0 - sigma))
        pre_grad = (upstream * gate_values * slope).astype(jnp.bfloat16)
        slot_grad = jnp.dot(pre_grad, weight[expert].T, preferred_element_type=jnp.float32).astype(jnp.bfloat16)
        weight_list.append(jnp.dot(slot_rows.T, pre_grad, preferred_element_type=jnp.float32))
        grad_tokens = jnp.where(chosen[:, None], slot_grad[rows], grad_tokens)
        grad_gate = jnp.where(chosen, slot_gate_grad[rows], grad_gate)
    activated = jnp.stack(activated_list, axis=0)
    grad_weight = jnp.stack(weight_list, axis=0)
    return activated, grad_tokens, grad_gate, grad_weight
```

```python
import jax
import jax.numpy as jnp
from jax import lax
from jax.experimental import pallas as pl
from jax.experimental.pallas import tpu as pltpu
from jax.sharding import PartitionSpec as P

CAP = 640
TOK = 1024
D = 3584
F = 1024
HALF = 512
ROWS = 112
PLANE = 1792
BLK = 256
NBLK = D // BLK
MESH = pl.DeviceIdType.MESH
F32 = jnp.float32
BF16 = jnp.bfloat16


def place():
    d, e = lax.axis_index("dp"), lax.axis_index("expert")
    core, z, y, x_lo = d % 2, (d // 2) % 4, (d // 8) % 4, d // 32
    a = y + core * (z - y)
    b = z + core * (y - z)
    return 2 * e + x_lo, a, b, core


def device(x, a, b, core):
    x, a, b = x % 4, a % 4, b % 4
    y = a + core * (b - a)
    z = b + core * (a - b)
    return (((x % 2) * 4 + y) * 4 + z) * 2 + core, x // 2


def sibling(x, a, b, core):
    return device(x, b, a, 1 - core)


def chunk_at(a, b, core):
    a, b = a % 4, b % 4
    y = a + core * (b - a)
    z = b + core * (a - b)
    return pl.ds(pl.multiple_of((y * 4 + z) * ROWS, 16), ROWS)


def enter(x, a, b, core):
    barrier = pltpu.get_barrier_semaphore()
    peers = [sibling(x, a, b, core)]
    for o in (1, 2, 3):
        peers += [device(x + o, a, b, core), device(x, a + o, b, core), device(x, a, b + o, core)]
    for peer in peers:
        pl.semaphore_signal(barrier, inc=1, device_id=peer, device_id_type=MESH)
    pl.semaphore_wait(barrier, len(peers))


def send(src, dst, send_sem, recv_sem, to):
    pltpu.make_async_remote_copy(
        src_ref=src, dst_ref=dst, send_sem=send_sem, recv_sem=recv_sem, device_id=to, device_id_type=MESH
    ).start()


def arrived(ref, sem):
    pltpu.make_async_copy(ref, ref, sem).wait()


def order(j):
    return j + j // 2 - 2 * (j // 3)


def gather_kernel(
    w_ref, owner_ref, gate_ref, x_hbm, cot_hbm,
    w_out, xt_out, p_out, act_out, ggs_out,
    W, X, XS, XT, Q, pre, cot, act, ggs, gs, A32, B32,
    s_loc, s_first, r_first, s_x, r_x, s_a, r_a, s_b, r_b, s_sib, r_sib, s_cot, r_cot, s_out,
):
    x, a, b, core = place()
    e, xl = x // 2, x % 2
    sib = sibling(x, a, b, core)

    load_x = pltpu.make_async_copy(x_hbm, X, s_loc.at[0])
    load_x.start()
    load_cot = []
    for h in (0, 1):
        load_cot.append(
            pltpu.make_async_copy(
                cot_hbm.at[0, pl.ds(pl.multiple_of(e * CAP, 16), CAP), pl.ds(h * HALF, HALF)],
                cot.at[e, h],
                s_loc.at[1 + h],
            )
        )
        load_cot[-1].start()
    enter(x, a, b, core)

    left, right = w_ref[0, :, :HALF].astype(F32), w_ref[0, :, HALF:].astype(F32)
    B32[...] = jnp.where(core == 0, right, left)
    swap = pltpu.make_async_remote_copy(
        src_ref=B32,
        dst_ref=A32.at[pl.ds(pl.multiple_of(core * 56, 8), 56)],
        send_sem=s_first.at[0],
        recv_sem=r_first.at[0],
        device_id=sib,
        device_id_type=MESH,
    )
    swap.start()
    A32[pl.ds(pl.multiple_of(core * 56, 8), 56), :] = jnp.where(core == 0, left, right)
    swap.wait()
    mine = chunk_at(a, b, core)
    W[core, e, xl, mine, :] = A32[...].astype(BF16)

    def plane(j):
        xj = (x + order(j)) % 4
        return W.at[core, xj // 2, xj % 2]

    def to_sibling(j, ref):
        send(ref, ref, s_sib.at[j], r_sib.at[j], sib)

    def send_a(j):
        ref = plane(j).at[mine, :]
        for s in (1, 3, 2):
            send(ref, ref, s_a.at[j, s - 1], r_a.at[j, 3 - s], device(x, a + s, b, core))
        to_sibling(j, ref)

    def send_b(j, r):
        ref = plane(j).at[chunk_at(a + r, b, core), :]
        for s in (1, 3, 2):
            send(ref, ref, s_b.at[j, s - 1, r], r_b.at[j, 3 - s, r], device(x, a, b + s, core))

    ref = W.at[core, e, xl, mine, :]
    for s in (1, 3, 2):
        send(ref, ref, s_x.at[s - 1], r_x.at[3 - s], device(x + s, a, b, core))
    send_a(0)
    send_b(0, 0)

    owner = jnp.broadcast_to(owner_ref[...], (8, TOK)).astype(F32)
    upper = (
        lax.broadcasted_iota(jnp.int32, (TOK, TOK), 0) <= lax.broadcasted_iota(jnp.int32, (TOK, TOK), 1)
    ).astype(BF16)
    ones = jnp.dot(owner.astype(BF16), upper, preferred_element_type=F32)
    token = lax.broadcasted_iota(jnp.int32, (8, TOK), 1).astype(F32)
    slot = jnp.where(owner > 0.5, CAP + ones - 1.0, token - ones)[:1].astype(jnp.int32)

    def one_hot(i, carry):
        rows = lax.broadcasted_iota(jnp.int32, (64, TOK), 0) + i * 64
        Q[pl.ds(pl.multiple_of(i * 64, 64), 64), :] = (rows == slot).astype(F32).astype(BF16)
        return carry

    lax.fori_loop(0, 2 * CAP // 64, one_hot, 0)
    gs[...] = lax.dot_general(
        Q[...],
        jnp.broadcast_to(gate_ref[...], (128, TOK)),
        (((1,), (1,)), ((), ())),
        preferred_element_type=F32,
    )
    pre[...] = jnp.zeros_like(pre)

    partner = device(x + 2, a, b, core)
    for h in (0, 1):
        send(
            cot_hbm.at[0, pl.ds(pl.multiple_of((1 - e) * CAP, 16), CAP), pl.ds(h * HALF, HALF)],
            cot.at[e, h],
            s_cot.at[h],
            r_cot.at[h],
            partner,
        )

    for o in (1, 3, 2):
        ref = plane(0).at[chunk_at(a + o, b, core), :]
        arrived(ref, r_a.at[0, o - 1])
        send_b(0, o)
        to_sibling(0, ref)
    for j in (1, 2, 3):
        arrived(plane(j).at[mine, :], r_x.at[order(j) - 1])
        send_a(j)
    load_x.wait()

    def dispatch(c):
        half, part = c // 7, c % 7
        cols = pl.ds(pl.multiple_of(c * BLK, BLK), BLK)
        inner = pl.ds(pl.multiple_of(part * BLK, BLK), BLK)
        block = X[:, cols]
        for k in (0, 1):
            rows = jnp.dot(Q[k * CAP : (k + 1) * CAP, :], block, preferred_element_type=F32)
            XS[k, half, :, inner] = rows.astype(BF16)
            XT[k, half, inner, :] = rows.T.astype(BF16)

    def forward(j, h):
        xj = (x + order(j)) % 4
        ej, xlj = xj // 2, xj % 2
        pre[ej, h] += jnp.dot(XS[ej, xlj], W[h, ej, xlj], preferred_element_type=F32)

    def pointwise(k):
        def tile(i, carry):
            rows = pl.ds(pl.multiple_of(i * 32, 32), 32)
            gate = gs[pl.ds(pl.multiple_of(k * CAP + i * 32, 32), 32), :]
            gate = jnp.concatenate([gate] * 4, axis=1)
            total = jnp.zeros((32, 1), F32)
            for h in (0, 1):
                z = pre[k, h, rows, :]
                s = jax.nn.sigmoid(z)
                shaped = z * s
                up = cot[k, h, rows, :].astype(F32)
                act[k, rows, h * HALF : (h + 1) * HALF] = (gate * shaped).astype(BF16)
                total += jnp.sum(up * shaped, axis=1, keepdims=True)
                cot[k, h, rows, :] = (up * gate * (s * (1.0 + z * (1.0 - s)))).astype(BF16)
            ggs[k, rows, :] = jnp.broadcast_to(total, (32, 128)).astype(BF16)
            return carry

        lax.fori_loop(0, CAP // 32, tile, 0)

    def step(j, carry):
        for r in (0, 1, 2, 3):

            @pl.when(j == 0)
            def _():
                def some(c, carry):
                    dispatch(c)
                    return carry

                lax.fori_loop((0, 4, 8, 11)[r], (4, 8, 11, 14)[r], some, 0)

            if r in (0, 2):

                @pl.when(j > 0)
                def _():
                    forward(j - 1, r // 2)

            if r == 1:

                @pl.when(j < 3)
                def _():
                    send_b(j + 1, 0)
                    for o in (1, 3, 2):
                        ref = plane(j + 1).at[chunk_at(a + o, b, core), :]
                        arrived(ref, r_a.at[j + 1, o - 1])
                        send_b(j + 1, o)
                        to_sibling(j + 1, ref)

            for o in (1, 3, 2):
                rr = (0, 1, 3, 2)[r]
                ref = plane(j).at[chunk_at(a + rr, b + o, core), :]
                arrived(ref, r_b.at[j, o - 1, rr])
                to_sibling(j, ref)
        xj = (x + order(j)) % 4
        arrived(W.at[1 - core, xj // 2, xj % 2], r_sib.at[j])
        for h in (0, 1):
            pltpu.make_async_copy(
                W.at[h, xj // 2, xj % 2], w_out.at[h, xj // 2, xj % 2], s_out.at[2 * j + h]
            ).start()
        return carry

    lax.fori_loop(0, 4, step, 0)
    save_xt = pltpu.make_async_copy(XT, xt_out, s_loc.at[0])
    save_xt.start()
    for k in load_cot:
        k.wait()
    pointwise(e)
    forward(3, 0)
    forward(3, 1)
    for h in (0, 1):
        arrived(cot.at[1 - e, h], r_cot.at[h])
    pointwise(1 - e)
    saves = [
        pltpu.make_async_copy(cot, p_out, s_loc.at[1]),
        pltpu.make_async_copy(act, act_out, s_loc.at[2]),
        pltpu.make_async_copy(ggs, ggs_out, s_loc.at[3]),
    ]
    for k in saves:
        k.start()
    for s in (0, 1, 2):
        arrived(W.at[core, e, xl, mine, :], s_x.at[s])
    for h in (0, 1):
        arrived(cot_hbm.at[0, pl.ds(0, CAP), pl.ds(0, HALF)], s_cot.at[h])

    def drain(j, carry):
        for s in (0, 1, 2):
            arrived(plane(j).at[mine, :], s_a.at[j, s])
            for r in (0, 1, 2, 3):
                arrived(plane(j).at[mine, :], s_b.at[j, s, r])
        arrived(plane(j), s_sib.at[j])
        for h in (0, 1):
            arrived(W.at[h, 0, 0], s_out.at[2 * j + h])
        return carry

    lax.fori_loop(0, 4, drain, 0)
    save_xt.wait()
    for k in saves:
        k.wait()


def reduce_kernel(
    owner_ref, p_hbm, xt_hbm, w_hbm, act_hbm, ggs_hbm,
    act_out, tok_out, gate_out, wg_out,
    PG, XT, WB, QT, GG, SB, RS, OWN, S, KB, RB, SA, RA, SX, RX, KA, FIN, SG, TB,
    s_in, s_xt, s_w, s_sib, r_sib, s_b, r_b, s_a, r_a, s_x, r_x, s_fin, r_fin, s_act, r_act, s_t,
):
    x, a, b, core = place()
    e = x // 2
    sib = sibling(x, a, b, core)

    def target(j):
        return (x + 2 + j - 3 * (j // 2) + 2 * (j // 3)) % 4

    def load_xt(j):
        t = target(j)
        return pltpu.make_async_copy(xt_hbm.at[t // 2, t % 2], XT.at[j % 2], s_xt.at[j % 2])

    def load_w(c):
        return pltpu.make_async_copy(
            w_hbm.at[:, :, c // 7, pl.ds(pl.multiple_of((c % 7) * BLK, BLK), BLK), :], WB.at[c % 2], s_w.at[c % 2]
        )

    load_p = pltpu.make_async_copy(p_hbm, PG, s_in.at[0])
    load_p.start()
    load_xt(0).start()
    load_g = pltpu.make_async_copy(ggs_hbm, GG, s_in.at[1])
    load_g.start()
    load_w(0).start()
    enter(x, a, b, core)

    half_rows = pl.ds(pl.multiple_of(e * CAP, 16), CAP)
    keep_act = pltpu.make_async_copy(act_hbm.at[e], act_out.at[0, half_rows, :], s_in.at[2])
    keep_act.start()
    load_p.wait()

    def grad_tokens(c):
        load_w(c).wait()

        @pl.when(c < NBLK - 1)
        def _():
            load_w(c + 1).start()

        for k in (0, 1):
            slots = lax.dot_general(
                PG[k, 0], WB[c % 2, 0, k], (((1,), (1,)), ((), ())), preferred_element_type=F32
            ) + lax.dot_general(PG[k, 1], WB[c % 2, 1, k], (((1,), (1,)), ((), ())), preferred_element_type=F32)
            SG[k * CAP : (k + 1) * CAP, :] = slots.astype(BF16)

        @pl.when(c >= 2)
        def _():
            arrived(TB.at[c % 2], s_t.at[c % 2])

        TB[c % 2] = jnp.dot(QT[...], SG[...], preferred_element_type=F32).astype(BF16)
        pltpu.make_async_copy(
            TB.at[c % 2], tok_out.at[:, pl.ds(pl.multiple_of(c * BLK, BLK), BLK)], s_t.at[c % 2]
        ).start()

    def some_tokens(first, last):
        def one(c, carry):
            grad_tokens(c)
            return carry

        lax.fori_loop(first, last, one, 0)

    def finish_b(j):
        for r in (1, 3, 2, 0):
            total = KB[j % 2, r]
            for o in (1, 2, 3):
                arrived(RB.at[j, o - 1, r], r_b.at[j, o - 1, r])
                total += RB[j, o - 1, r].astype(F32)
            if r:
                SA[j, r - 1] = total.astype(BF16)
                send(SA.at[j, r - 1], RA.at[j, 3 - r], s_a.at[j, r - 1], r_a.at[j, 3 - r], device(x, a + r, b, core))
            else:
                KA[j % 2] = total

    def finish_a(j):
        total = KA[j % 2]
        for o in (1, 2, 3):
            arrived(RA.at[j, o - 1], r_a.at[j, o - 1])
            total += RA[j, o - 1].astype(F32)
        return total

    def finish_x(j):
        away = (target(j) - x + 4) % 4
        SX[j] = finish_a(j).astype(BF16)
        send(SX.at[j], RX.at[3 - away], s_x.at[j], r_x.at[3 - away], device(x + away, a, b, core))

    def step(j, carry):
        t = target(j)
        load_xt(j).wait()

        @pl.when(j < 3)
        def _():
            load_xt(j + 1).start()

        @pl.when(j >= 2)
        def _():
            arrived(SB.at[j % 2], s_sib.at[j % 2])

        def theirs(i, carry):
            rows = pl.ds(pl.multiple_of(i * 448, 64), 448)
            SB[j % 2, rows, :] = jnp.dot(
                XT[j % 2, rows, :], PG[t // 2, 1 - core], preferred_element_type=F32
            ).astype(BF16)
            return carry

        def ours(i, carry):
            rows = pl.ds(pl.multiple_of(i * 448, 64), 448)
            OWN[rows, :] = jnp.dot(XT[j % 2, rows, :], PG[t // 2, core], preferred_element_type=F32)
            return carry

        lax.fori_loop(0, 4, theirs, 0)
        send(SB.at[j % 2], RS.at[j], s_sib.at[j % 2], r_sib.at[j], sib)
        lax.fori_loop(0, 4, ours, 0)

        @pl.when(j == 0)
        def _():
            owner = jnp.broadcast_to(owner_ref[...], (TOK, 128)).astype(F32)
            lower = (
                lax.broadcasted_iota(jnp.int32, (TOK, TOK), 0) >= lax.broadcasted_iota(jnp.int32, (TOK, TOK), 1)
            ).astype(BF16)
            ones = jnp.dot(lower, owner.astype(BF16), preferred_element_type=F32)
            token = lax.broadcasted_iota(jnp.int32, (TOK, 128), 0).astype(F32)
            slot = jnp.where(owner > 0.5, CAP + ones - 1.0, token - ones).astype(jnp.int32)
            for i in range(10):
                column = lax.broadcasted_iota(jnp.int32, (TOK, 128), 1) + i * 128
                QT[:, i * 128 : (i + 1) * 128] = (column == slot).astype(F32).astype(BF16)

        arrived(RS.at[j], r_sib.at[j])
        for r in (1, 3, 2, 0):
            for o in (2, 1, 3, 0):
                rows = chunk_at(a + r, b + o, core)
                total = OWN[rows, :] + RS[j, rows, :].astype(F32)
                if o:
                    S[j, o - 1, r] = total.astype(BF16)
                    send(
                        S.at[j, o - 1, r],
                        RB.at[j, 3 - o, r],
                        s_b.at[j, o - 1, r],
                        r_b.at[j, 3 - o, r],
                        device(x, a, b + o, core),
                    )
                else:
                    KB[j % 2, r] = total

        @pl.when(j == 0)
        def _():
            send(act_hbm.at[1 - e], act_out.at[0, half_rows, :], s_act.at[0], r_act.at[0], device(x + 2, a, b, core))

        some_tokens(3 * j, 3 * j + 3)

        @pl.when(j >= 1)
        def _():
            finish_b(j - 1)

        @pl.when(j >= 2)
        def _():
            finish_x(j - 2)

        return carry

    lax.fori_loop(0, 4, step, 0)
    finish_x(2)
    some_tokens(12, 14)
    load_g.wait()
    flat = jnp.concatenate([GG[0], GG[1]], axis=0)
    gate_out[...] = jnp.dot(QT[...], flat, preferred_element_type=F32)[:, :1].astype(BF16)
    finish_b(3)
    total = finish_a(3)
    for o in (1, 3, 2):
        arrived(RX.at[o - 1], r_x.at[o - 1])
        total += RX[o - 1].astype(F32)
    FIN[0] = total
    swap = pltpu.make_async_remote_copy(
        src_ref=FIN.at[0, pl.ds(pl.multiple_of((1 - core) * 56, 8), 56), :],
        dst_ref=FIN.at[1, pl.ds(pl.multiple_of((1 - core) * 56, 8), 56), :],
        send_sem=s_fin.at[0],
        recv_sem=r_fin.at[0],
        device_id=sib,
        device_id_type=MESH,
    )
    swap.start()
    swap.wait_send()
    arrived(FIN.at[1, pl.ds(pl.multiple_of(core * 56, 8), 56), :], r_fin.at[0])
    kept = FIN[0, pl.ds(pl.multiple_of(core * 56, 8), 56), :]
    came = FIN[1, pl.ds(pl.multiple_of(core * 56, 8), 56), :]
    wg_out[0, :, :HALF] = jnp.where(core == 0, kept, came)
    wg_out[0, :, HALF:] = jnp.where(core == 0, came, kept)

    keep_act.wait()
    arrived(act_hbm.at[0], s_act.at[0])
    arrived(act_out.at[0, pl.ds(pl.multiple_of((1 - e) * CAP, 16), CAP), :], r_act.at[0])
    for i in (0, 1):
        arrived(TB.at[i], s_t.at[i])
        arrived(SB.at[i], s_sib.at[i])

    def drain(j, carry):
        for o in (0, 1, 2):
            arrived(SA.at[j, o], s_a.at[j, o])
            for r in (0, 1, 2, 3):
                arrived(S.at[j, o, r], s_b.at[j, o, r])
        return carry

    lax.fori_loop(0, 4, drain, 0)
    for j in (0, 1, 2):
        arrived(SX.at[j], s_x.at[j])


def body(tokens, assignment, gate, weight, cotangent):
    ANY, VMEM = pl.BlockSpec(memory_space=pl.ANY), pl.BlockSpec(memory_space=pltpu.VMEM)
    DMA = pltpu.SemaphoreType.DMA
    shape = jax.ShapeDtypeStruct
    full_w, xt, p, act, ggs = pl.pallas_call(
        gather_kernel,
        out_shape=(
            shape((2, 2, 2, PLANE, HALF), BF16),
            shape((2, 2, PLANE, CAP), BF16),
            shape((2, 2, CAP, HALF), BF16),
            shape((2, CAP, F), BF16),
            shape((2, CAP, 128), BF16),
        ),
        in_specs=[VMEM, VMEM, VMEM, ANY, ANY],
        out_specs=(ANY,) * 5,
        scratch_shapes=[
            pltpu.VMEM((2, 2, 2, PLANE, HALF), BF16),
            pltpu.VMEM((TOK, D), BF16),
            pltpu.VMEM((2, 2, CAP, PLANE), BF16),
            pltpu.VMEM((2, 2, PLANE, CAP), BF16),
            pltpu.VMEM((2 * CAP, TOK), BF16),
            pltpu.VMEM((2, 2, CAP, HALF), F32),
            pltpu.VMEM((2, 2, CAP, HALF), BF16),
            pltpu.VMEM((2, CAP, F), BF16),
            pltpu.VMEM((2, CAP, 128), BF16),
            pltpu.VMEM((2 * CAP, 128), F32),
            pltpu.VMEM((ROWS, HALF), F32),
            pltpu.VMEM((56, HALF), F32),
            DMA((4,)), DMA((1,)), DMA((1,)), DMA((3,)), DMA((3,)), DMA((4, 3)), DMA((4, 3)),
            DMA((4, 3, 4)), DMA((4, 3, 4)), DMA((4,)), DMA((4,)), DMA((2,)), DMA((2,)), DMA((8,)),
        ],
        compiler_params=pltpu.CompilerParams(collective_id=1, has_side_effects=True, vmem_limit_bytes=62 * 2**20),
        name="gather_forward",
    )(weight, assignment.reshape(1, TOK), gate.reshape(1, TOK), tokens, cotangent)
    activated, grad_tokens, grad_gate, grad_weight = pl.pallas_call(
        reduce_kernel,
        out_shape=(
            shape((1, 2 * CAP, F), BF16),
            shape((TOK, D), BF16),
            shape((TOK, 1), BF16),
            shape((1, 56, F), F32),
        ),
        in_specs=[VMEM, ANY, ANY, ANY, ANY, ANY],
        out_specs=(ANY, ANY, VMEM, VMEM),
        scratch_shapes=[
            pltpu.VMEM((2, 2, CAP, HALF), BF16),
            pltpu.VMEM((2, PLANE, CAP), BF16),
            pltpu.VMEM((2, 2, 2, BLK, HALF), BF16),
            pltpu.VMEM((TOK, 2 * CAP), BF16),
            pltpu.VMEM((2, CAP, 128), BF16),
            pltpu.VMEM((2, PLANE, HALF), BF16),
            pltpu.VMEM((4, PLANE, HALF), BF16),
            pltpu.VMEM((PLANE, HALF), F32),
            pltpu.VMEM((4, 3, 4, ROWS, HALF), BF16),
            pltpu.VMEM((2, 4, ROWS, HALF), F32),
            pltpu.VMEM((4, 3, 4, ROWS, HALF), BF16),
            pltpu.VMEM((4, 3, ROWS, HALF), BF16),
            pltpu.VMEM((4, 3, ROWS, HALF), BF16),
            pltpu.VMEM((3, ROWS, HALF), BF16),
            pltpu.VMEM((3, ROWS, HALF), BF16),
            pltpu.VMEM((2, ROWS, HALF), F32),
            pltpu.VMEM((2, ROWS, HALF), F32),
            pltpu.VMEM((2 * CAP, BLK), BF16),
            pltpu.VMEM((2, TOK, BLK), BF16),
            DMA((3,)), DMA((2,)), DMA((2,)), DMA((2,)), DMA((4,)), DMA((4, 3, 4)), DMA((4, 3, 4)),
            DMA((4, 3)), DMA((4, 3)), DMA((3,)), DMA((3,)), DMA((1,)), DMA((1,)), DMA((1,)), DMA((1,)), DMA((2,)),
        ],
        compiler_params=pltpu.CompilerParams(collective_id=2, has_side_effects=True, vmem_limit_bytes=62 * 2**20),
        name="backward_reduce",
    )(assignment, p, xt, full_w, act, ggs)
    return activated, grad_tokens, grad_gate.reshape(TOK), grad_weight


def solution(mesh):
    placed = (
        P(("dp", "expert"), None),
        P(("dp", "expert"), None),
        P(("dp", "expert")),
        P("expert", "dp", None),
        P("expert", "dp", None),
    )
    return jax.shard_map(
        body,
        mesh=mesh,
        in_specs=placed,
        out_specs=(
            P("expert", "dp", None),
            P(("dp", "expert"), None),
            P(("dp", "expert")),
            P("expert", "dp", None),
        ),
        check_vma=False,
    )
```

```python
import jax
import jax.numpy as jnp
from jax import lax
from jax.experimental import pallas as pl
from jax.experimental.pallas import tpu as pltpu
from jax.sharding import PartitionSpec as P

CAP = 640
TOK = 1024
D = 3584
F = 1024
HALF = 512
ROWS = 112
PLANE = 1792
BLK = 512
NBLK = D // BLK
EARLY = 3
MESH = pl.DeviceIdType.MESH
F32 = jnp.float32
BF16 = jnp.bfloat16


def place():
    d, e = lax.axis_index("dp"), lax.axis_index("expert")
    core, z, y, x_lo = d % 2, (d // 2) % 4, (d // 8) % 4, d // 32
    a = y + core * (z - y)
    b = z + core * (y - z)
    return e, x_lo, a, b, core


def device(x, a, b, core):
    x, a, b = x % 4, a % 4, b % 4
    y = a + core * (b - a)
    z = b + core * (a - b)
    return (((x % 2) * 4 + y) * 4 + z) * 2 + core, x // 2


def chunk_row(a, b, core):
    a, b = a % 4, b % 4
    y = a + core * (b - a)
    z = b + core * (a - b)
    return (y * 4 + z) * ROWS


def rows_at(start, size, by=16):
    return pl.ds(pl.multiple_of(start, by), size)


def copy_to(src, dst, send_sem, recv_sem, to):
    return pltpu.make_async_remote_copy(
        src_ref=src, dst_ref=dst, send_sem=send_sem, recv_sem=recv_sem, device_id=to, device_id_type=MESH
    )


def send(*args):
    copy_to(*args).start()


def arrived(ref, sem):
    pltpu.make_async_copy(ref, ref, sem).wait()


def nn(p, q):
    return jnp.dot(p, q, preferred_element_type=F32)


def nt(p, q):
    return lax.dot_general(p, q, (((1,), (1,)), ((), ())), preferred_element_type=F32)


def tn(p, q):
    return lax.dot_general(p, q, (((0,), (0,)), ((), ())), preferred_element_type=F32)


def loop(first, last, f):
    def one(i, carry):
        f(i)
        return carry

    lax.fori_loop(first, last, one, 0)


def one_hot_rows(owner_ref, Q):
    owner = jnp.broadcast_to(owner_ref[...], (8, TOK)).astype(F32)
    upper = (
        lax.broadcasted_iota(jnp.int32, (TOK, TOK), 0) <= lax.broadcasted_iota(jnp.int32, (TOK, TOK), 1)
    ).astype(BF16)
    ones = nn(owner.astype(BF16), upper)
    token = lax.broadcasted_iota(jnp.int32, (8, TOK), 1).astype(F32)
    slot = jnp.where(owner > 0.5, CAP + ones - 1.0, token - ones)[:1].astype(jnp.int32)

    def some(i):
        rows = lax.broadcasted_iota(jnp.int32, (64, TOK), 0) + i * 64
        Q[rows_at(i * 64, 64), :] = (rows == slot).astype(F32).astype(BF16)

    loop(0, 2 * CAP // 64, some)


def main_kernel(
    w_ref, owner_ref, gate_ref, x_hbm, cot_hbm,
    act_out, tok_out, sg_out, gate_out, wg_out,
    W, XS, Q, pre, PG, ACT, ggs, gs,
    SB, RSB, OWN, S, RB, T2, KB, SA, RA, SX, RX, KA, MINE, FIN, SG,
    s_loc, s_blk, s_first, r_first, s_x, r_x, s_a, r_a, s_b, r_b, s_sib, r_sib, s_cot, r_cot,
    s_sb, r_sb, credit, s_ra, r_ra, s_rb, r_rb, s_rx, r_rx, s_fin, r_fin, s_act, r_act, s_sg, s_tok,
):
    e, xl, a, b, core = place()
    x = 2 * e + xl
    sib = device(x, b, a, 1 - core)
    half = pl.ds(pl.multiple_of(core * HALF, HALF), HALF)
    other = pl.ds(pl.multiple_of((1 - core) * HALF, HALF), HALF)

    def plane(j):
        ee = e + (j // 2) * (1 - 2 * e)
        flip = ((j + 1) // 2) % 2
        return ee, xl + flip * (1 - 2 * xl)

    def target(j):
        return plane(j + 1 - 2 * (j % 2))

    def away(p):
        return (2 * p[0] + p[1] - x + 4) % 4

    def block_cols(c):
        return pl.ds(pl.multiple_of(c * BLK, BLK), BLK)

    def block_of(i):
        return (i + 3 * xl) % NBLK

    def load_x(i):
        return pltpu.make_async_copy(x_hbm.at[:, block_cols(block_of(i))], SG.at[i % 2, :TOK], s_blk.at[i % 2])

    load_x(0).start()
    load_x(1).start()
    load_cot = pltpu.make_async_copy(cot_hbm.at[0, rows_at(e * CAP, CAP), :], PG.at[e], s_loc.at[0])
    load_cot.start()

    barrier = pltpu.get_barrier_semaphore()
    peers = [sib]
    for o in (1, 2, 3):
        peers.append(device(x + o, a, b, core))
    for o in (1, 3):
        peers += [device(x, a + o, b, core), device(x, a, b + o, core)]
    for peer in peers:
        pl.semaphore_signal(barrier, inc=1, device_id=peer, device_id_type=MESH)
    pl.semaphore_wait(barrier, len(peers))

    left, right = w_ref[0, :, :HALF].astype(F32), w_ref[0, :, HALF:].astype(F32)
    FIN[1, :56] = jnp.where(core == 0, right, left)
    swap = copy_to(FIN.at[1, :56], FIN.at[0, rows_at(core * 56, 56, 8), :], s_first.at[0], r_first.at[0], sib)
    swap.start()
    FIN[0, rows_at(core * 56, 56, 8), :] = jnp.where(core == 0, left, right)
    swap.wait()

    def piece(j, r, o):
        ee, ll = plane(j)
        return W.at[ee, rows_at(ll * PLANE + chunk_row(a + r, b + o, core), ROWS), half]

    def to_sibling(j, ref):
        send(ref, ref, s_sib.at[j], r_sib.at[j], sib)

    mine = piece(0, 0, 0)
    W[e, rows_at(xl * PLANE + chunk_row(a, b, core), ROWS), half] = FIN[0].astype(BF16)

    def send_a(j):
        ref = piece(j, 0, 0)
        for s in (1, 3):
            send(ref, ref, s_a.at[j, s - 1], r_a.at[j, 3 - s], device(x, a + s, b, core))
        to_sibling(j, ref)

    def take_a(j):
        for o in (1, 3):
            arrived(piece(j, o, 0), r_a.at[j, o - 1])
            to_sibling(j, piece(j, o, 0))
        o = 3 - 2 * (j % 2)
        ref = piece(j, o, 0)
        send(ref, ref, s_a.at[j, 1], r_a.at[j, 1], device(x, a - o, b, core))

    def far_a(j):
        arrived(piece(j, 2, 0), r_a.at[j, 1])
        to_sibling(j, piece(j, 2, 0))

    def send_b(j, r):
        ref = piece(j, r, 0)
        for s in (1, 3):
            send(ref, ref, s_b.at[j, s - 1, r], r_b.at[j, 3 - s, r], device(x, a, b + s, core))

    def take_b(j, r):
        for o in (1, 3):
            arrived(piece(j, r, o), r_b.at[j, o - 1, r])
            to_sibling(j, piece(j, r, o))
        o = 3 if r < 2 else 1
        ref = piece(j, r, o)
        send(ref, ref, s_b.at[j, 1, r], r_b.at[j, 1, r], device(x, a, b - o, core))

    def far_b(j, r):
        arrived(piece(j, r, 2), r_b.at[j, 1, r])
        to_sibling(j, piece(j, r, 2))

    for s in (1, 3, 2):
        send(mine, mine, s_x.at[s - 1], r_x.at[3 - s], device(x + s, a, b, core))
    send_a(0)
    send_b(0, 0)

    one_hot_rows(owner_ref, Q)
    g8 = gate_ref[...].astype(F32)
    gate_row = jnp.concatenate([g8[i : i + 1] for i in range(8)], axis=1)
    gs[...] = nt(Q[...], jnp.broadcast_to(gate_row, (128, TOK)).astype(BF16))

    take_a(0)
    send_b(0, 1)
    send_b(0, 3)
    partner = device(x + 2, a, b, core)
    theirs_rows = rows_at((1 - e) * CAP, CAP)
    send(cot_hbm.at[0, theirs_rows, :], PG.at[e], s_cot.at[0], r_cot.at[0], partner)
    for j in (1, 2, 3):
        arrived(piece(j, 0, 0), r_x.at[away(plane(j)) - 1])
        send_a(j)
    far_a(0)
    send_b(0, 2)

    def dispatch(i):
        load_x(i).wait()
        cols = block_cols(block_of(i))
        XS[:, cols] = nn(Q[...], SG[i % 2, :TOK]).astype(BF16)

        @pl.when(i < NBLK - 2)
        def _():
            load_x(i + 2).start()

    def slots_of(k, l):
        return XS[rows_at(k * CAP, CAP), pl.ds(pl.multiple_of(l * PLANE, 256), PLANE)]

    def forward(j, h):
        ee, ll = plane(j)
        cols = slice(h * HALF, (h + 1) * HALF)
        part = nn(slots_of(ee, ll), W[ee, rows_at(ll * PLANE, PLANE, 256), cols])
        pre[:, cols] = jnp.where(j % 2 == 0, part, pre[:, cols] + part)

    def pointwise(k):
        def tile(i):
            rows = rows_at(i * 64, 64, 64)
            gate = gs[rows_at(k * CAP + i * 64, 64, 64), :]
            gate = jnp.concatenate([gate] * 4, axis=1)
            total = jnp.zeros((64, 1), F32)
            for h in (0, 1):
                cols = slice(h * HALF, (h + 1) * HALF)
                z = pre[rows, cols]
                s = 0.5 + 0.5 * jnp.tanh(0.5 * z)
                shaped = z * s
                up = PG[k, rows, cols].astype(F32)
                ACT[rows, cols] = (gate * shaped).astype(BF16)
                total += jnp.sum(up * shaped, axis=1, keepdims=True)
                PG[k, rows, cols] = (up * gate * (s * (1.0 + z * (1.0 - s)))).astype(BF16)
            ggs[rows_at(k * CAP + i * 64, 64, 64), :] = jnp.broadcast_to(total, (64, 128))

        loop(0, CAP // 64, tile)

    def theirs(j):
        ee, ll = target(j)
        for i in (0, 1):
            part = XS[rows_at(ee * CAP, CAP), pl.ds(pl.multiple_of(ll * PLANE + i * 896, 128), 896)]
            SB[i * 896 : (i + 1) * 896, :] = tn(part, PG[ee, :, other]).astype(BF16)
        send(SB, RSB.at[j % 2], s_sb.at[0], r_sb.at[j % 2], sib)

    def ours(j):
        ee, ll = target(j)
        for i in (0, 1):
            part = XS[rows_at(ee * CAP, CAP), pl.ds(pl.multiple_of(ll * PLANE + i * 896, 128), 896)]
            OWN[i * 896 : (i + 1) * 896, :] = tn(part, PG[ee, :, half])

    def first_sends(j):
        arrived(RSB.at[j % 2], r_sb.at[j % 2])

        def summed(r, o):
            rows = rows_at(chunk_row(a + r, b + o, core), ROWS)
            return rows, OWN[rows, :] + RSB[j % 2, rows, :].astype(F32)

        for r in (0, 2, 1, 3):
            S[j % 2, 1, r] = summed(r, 2)[1].astype(BF16)
            s = 1 if r < 2 else 3
            send(S.at[j % 2, 1, r], T2.at[j, r], s_rb.at[j, 1, r], r_rb.at[j, 1, r], device(x, a, b + s, core))
        for r in (2, 0, 3, 1):
            s = 3 if r < 2 else 1
            S[j % 2, s - 1, r] = summed(r, s)[1].astype(BF16)
            send(
                S.at[j % 2, s - 1, r], RB.at[j, s // 2, r],
                s_rb.at[j, s - 1, r], r_rb.at[j, 3 - s, r], device(x, a, b + s, core),
            )
        for r in (0, 1, 2, 3):
            KB[j % 2, r] = summed(r, 0)[1]
            rows, total = summed(r, 1 if r < 2 else 3)
            OWN[rows, :] = total

    def relayed_sends(j):
        for r in (0, 2, 1, 3):
            s = 1 if r < 2 else 3
            arrived(T2.at[j, r], r_rb.at[j, 1, r])
            rows = rows_at(chunk_row(a + r, b + s, core), ROWS)
            S[j % 2, s - 1, r] = (OWN[rows, :] + T2[j, r].astype(F32)).astype(BF16)
            send(
                S.at[j % 2, s - 1, r], RB.at[j, s // 2, r],
                s_rb.at[j, s - 1, r], r_rb.at[j, 3 - s, r], device(x, a, b + s, core),
            )

    def sent_b(j):
        for o in (0, 1, 2):
            for r in (0, 1, 2, 3):
                arrived(S.at[j % 2, o, r], s_rb.at[j, o, r])

    def sent_a(j):
        for s in (0, 1, 2):
            arrived(SA.at[j % 2, s], s_ra.at[j, s])

    def finish_b(j):
        def total(r):
            for o in (1, 3):
                arrived(RB.at[j, 1 if o == 3 else 0, r], r_rb.at[j, o - 1, r])
            return KB[j % 2, r] + RB[j, 0, r].astype(F32) + RB[j, 1, r].astype(F32)

        @pl.when(j >= 2)
        def _():
            sent_a(j - 2)

        s = 1 + 2 * (j % 2)
        SA[j % 2, 1] = total(2).astype(BF16)
        send(SA.at[j % 2, 1], RA.at[j, 1], s_ra.at[j, 1], r_ra.at[j, 1], device(x, a + s, b, core))
        for r in (1, 3, 0):
            KB[j % 2, r] = total(r)
        t = 4 - s
        SA[j % 2, t - 1] = KB[j % 2, t].astype(BF16)
        send(SA.at[j % 2, t - 1], RA.at[j, 3 - t], s_ra.at[j, t - 1], r_ra.at[j, 3 - t], device(x, a + t, b, core))

    def relay_a(j):
        s = 1 + 2 * (j % 2)
        arrived(RA.at[j, 1], r_ra.at[j, 1])
        SA[j % 2, s - 1] = (KB[j % 2, s] + RA[j, 1].astype(F32)).astype(BF16)
        send(SA.at[j % 2, s - 1], RA.at[j, 3 - s], s_ra.at[j, s - 1], r_ra.at[j, 3 - s], device(x, a + s, b, core))
        KA[j % 2] = KB[j % 2, 0]

    def finish_a(j):
        total = KA[j % 2]
        for o in (1, 3):
            arrived(RA.at[j, o - 1], r_ra.at[j, o - 1])
            total += RA[j, o - 1].astype(F32)
        return total

    def finish_x(j):
        o = away(target(j))
        SX[o - 1] = finish_a(j).astype(BF16)
        send(SX.at[o - 1], RX.at[3 - o], s_rx.at[o - 1], r_rx.at[3 - o], device(x + o, a, b, core))

    def slot_grad(k, c):
        cols = block_cols(c)

        @pl.when(c >= 2)
        def _():
            arrived(SG.at[c % 2, :CAP], s_sg.at[c % 2])

        SG[c % 2, :CAP] = nt(PG[k], W[k, cols, :]).astype(BF16)
        pltpu.make_async_copy(SG.at[c % 2, :CAP], sg_out.at[k, :, cols], s_sg.at[c % 2]).start()

    def slot_grads(k, first, last):
        loop(first, last, lambda c: slot_grad(k, c))

    def drain_sg():
        for i in (0, 1):
            arrived(SG.at[i, :CAP], s_sg.at[i])

    def gather_step(j):
        for i, r in enumerate((0, 1, 3, 2)):

            @pl.when(j == 0)
            def _():
                dispatch(i)

            if i == 0:

                @pl.when(j > 0)
                def _():
                    forward(j - 1, 0)

            if i == 1:

                @pl.when(j > 0)
                def _():
                    forward(j - 1, 1)

            if i == 2:

                @pl.when(j == 1)
                def _():
                    dispatch(4)
                    dispatch(5)

                @pl.when(j == 2)
                def _():
                    load_cot.wait()
                    pointwise(e)

            if i == 3:

                @pl.when(j == 1)
                def _():
                    dispatch(6)

                @pl.when(j == 2)
                def _():
                    theirs(0)

            take_b(j, r)

        @pl.when(j < 3)
        def _():
            send_b(j + 1, 0)
            take_a(j + 1)
            send_b(j + 1, 1)
            send_b(j + 1, 3)
            far_a(j + 1)
            send_b(j + 1, 2)

        @pl.when(j == 2)
        def _():
            ours(0)
            pltpu.make_async_copy(ACT, act_out.at[0, rows_at(e * CAP, CAP), :], s_loc.at[1]).start()

        @pl.when(j == 3)
        def _():
            first_sends(0)
            pl.semaphore_signal(credit, inc=1, device_id=sib, device_id_type=MESH)
            slot_grads(e, 0, 4)

        for r in (0, 1, 3, 2):
            far_b(j, r)

        @pl.when(j == 3)
        def _():
            slot_grads(e, 4, NBLK)

        ee, ll = plane(j)
        arrived(W.at[ee, rows_at(ll * PLANE, PLANE), other], r_sib.at[j])

    loop(0, 4, gather_step)
    drain_sg()

    def reduce_step(j):
        @pl.when(j > 0)
        def _():
            @pl.when(j >= 2)
            def _():
                relay_a(j - 2)
                sent_b(j - 2)

            first_sends(j)

            @pl.when(j == 1)
            def _():
                pl.semaphore_signal(credit, inc=1, device_id=sib, device_id_type=MESH)
                arrived(PG.at[1 - e], r_cot.at[0])
                arrived(ACT, s_loc.at[1])
                pointwise(1 - e)
                send(ACT, act_out.at[0, rows_at(e * CAP, CAP), :], s_act.at[0], r_act.at[0], partner)

        @pl.when(j < 3)
        def _():
            arrived(SB, s_sb.at[0])

            @pl.when(j >= 1)
            def _():
                pl.semaphore_wait(credit, 1)

            theirs(j + 1)

        @pl.when(j == 0)
        def _():
            forward(3, 0)

        @pl.when(j == 2)
        def _():
            slot_grads(1 - e, 0, 3)

        relayed_sends(j)

        @pl.when(j < 3)
        def _():
            ours(j + 1)

        @pl.when(j == 0)
        def _():
            forward(3, 1)

        @pl.when(j >= 1)
        def _():
            finish_b(j - 1)

        @pl.when(j == 3)
        def _():
            finish_x(0)

    loop(0, 4, reduce_step)
    slot_grads(1 - e, 3, 6)
    relay_a(2)
    MINE[...] = finish_a(1)
    slot_grads(1 - e, 6, NBLK)
    drain_sg()
    finish_b(3)
    finish_x(2)

    def early(c):
        for k in (0, 1):
            pltpu.make_async_copy(
                sg_out.at[k, :, block_cols(c)], SG.at[c % 2, k * CAP : (k + 1) * CAP], s_sg.at[c % 2]
            ).start()

    def combine(c):
        arrived(SG.at[c % 2], s_sg.at[c % 2])

        @pl.when(c >= 2)
        def _():
            arrived(RSB.at[c % 2, :TOK], s_tok.at[c % 2])

        RSB[c % 2, :TOK] = tn(Q[...], SG[c % 2]).astype(BF16)
        pltpu.make_async_copy(RSB.at[c % 2, :TOK], tok_out.at[:, block_cols(c)], s_tok.at[c % 2]).start()

        @pl.when(c + 2 < EARLY)
        def _():
            early(c + 2)

    early(0)
    early(1)
    combine(0)
    relay_a(3)
    loop(1, EARLY, combine)
    gg = ggs[...].T[:8].astype(BF16)
    row = nn(gg, Q[...])
    gate_out[...] = jnp.concatenate([row[:1, i * 128 : (i + 1) * 128] for i in range(8)], axis=0)
    finish_x(3)
    total = MINE[...]
    for o in (1, 2, 3):
        arrived(RX.at[o - 1], r_rx.at[o - 1])
        total += RX[o - 1].astype(F32)
    FIN[0] = total
    away_rows = rows_at((1 - core) * 56, 56, 8)
    kept_rows = rows_at(core * 56, 56, 8)
    last = copy_to(FIN.at[0, away_rows, :], FIN.at[1, away_rows, :], s_fin.at[0], r_fin.at[0], sib)
    last.start()
    last.wait_send()
    arrived(FIN.at[1, kept_rows, :], r_fin.at[0])
    kept, came = FIN[0, kept_rows, :], FIN[1, kept_rows, :]
    wg_out[0, :, :HALF] = jnp.where(core == 0, kept, came)
    wg_out[0, :, HALF:] = jnp.where(core == 0, came, kept)

    for s in (0, 1, 2):
        arrived(mine, s_x.at[s])
        arrived(SX.at[s], s_rx.at[s])
    arrived(cot_hbm.at[0, theirs_rows, :], s_cot.at[0])
    arrived(ACT, s_act.at[0])
    arrived(SB, s_sb.at[0])
    arrived(act_out.at[0, theirs_rows, :], r_act.at[0])
    for i in (0, 1):
        arrived(RSB.at[i, :TOK], s_tok.at[i])

    def drain(j):
        for s in (0, 1, 2):
            arrived(piece(j, 0, 0), s_a.at[j, s])
            for r in (0, 1, 2, 3):
                arrived(piece(j, 0, 0), s_b.at[j, s, r])
        ee, ll = plane(j)
        arrived(W.at[ee, rows_at(ll * PLANE, PLANE), half], s_sib.at[j])

        @pl.when(j >= 2)
        def _():
            sent_a(j)
            sent_b(j)

    loop(0, 4, drain)


def combine_kernel(
    owner_ref, gate_ref, sg_hbm, tok_hbm, act_hbm, wg_hbm,
    gate_out, tok_out, act_out, wg_out,
    Q, SG, TB, TV, AV, GV, s_sg, s_tok, s_in, s_out,
):
    def cols(c):
        return pl.ds(pl.multiple_of(c * BLK, BLK), BLK)

    def load(c):
        return [
            pltpu.make_async_copy(
                sg_hbm.at[k, :, cols(c)], SG.at[c % 2, k * CAP : (k + 1) * CAP], s_sg.at[c % 2, k]
            )
            for k in (0, 1)
        ]

    moves = [
        (act_hbm, AV, act_out),
        (tok_hbm, TV, tok_out.at[:, : EARLY * BLK]),
        (wg_hbm, GV, wg_out),
    ]
    moves = [
        (pltpu.make_async_copy(p, v, s_in.at[i]), pltpu.make_async_copy(v, q, s_out.at[i]))
        for i, (p, v, q) in enumerate(moves)
    ]
    for c in (EARLY, EARLY + 1):
        for k in load(c):
            k.start()
    for k, _ in moves:
        k.start()
    one_hot_rows(owner_ref, Q)
    gate_out[...] = gate_ref[...].astype(BF16)

    def combine(c):
        for k in load(c):
            k.wait()

        @pl.when(c >= EARLY + 2)
        def _():
            arrived(TB.at[c % 2], s_tok.at[c % 2])

        TB[c % 2] = tn(Q[...], SG[c % 2]).astype(BF16)
        pltpu.make_async_copy(TB.at[c % 2], tok_out.at[:, cols(c)], s_tok.at[c % 2]).start()

        @pl.when(c + 2 < NBLK)
        def _():
            for k in load(c + 2):
                k.start()

    loop(EARLY, EARLY + 1, combine)
    for k, m in moves:
        k.wait()
        m.start()
    loop(EARLY + 1, NBLK, combine)
    for i in (0, 1):
        arrived(TB.at[i], s_tok.at[i])
    for _, m in moves:
        m.wait()


def body(tokens, assignment, gate, weight, cotangent):
    ANY, VMEM = pl.BlockSpec(memory_space=pl.ANY), pl.BlockSpec(memory_space=pltpu.VMEM)
    DMA = pltpu.SemaphoreType.DMA
    shape = jax.ShapeDtypeStruct
    owner = assignment.reshape(1, TOK)
    act, tok, sg, grad_gate, grad_weight = pl.pallas_call(
        main_kernel,
        out_shape=(
            shape((1, 2 * CAP, F), BF16),
            shape((TOK, EARLY * BLK), BF16),
            shape((2, CAP, D), BF16),
            shape((8, 128), F32),
            shape((1, 56, F), F32),
        ),
        in_specs=[VMEM, VMEM, VMEM, ANY, ANY],
        out_specs=(ANY, ANY, ANY, VMEM, VMEM),
        scratch_shapes=[
            pltpu.VMEM((2, D, F), BF16),
            pltpu.VMEM((2 * CAP, D), BF16),
            pltpu.VMEM((2 * CAP, TOK), BF16),
            pltpu.VMEM((CAP, F), F32),
            pltpu.VMEM((2, CAP, F), BF16),
            pltpu.VMEM((CAP, F), BF16),
            pltpu.VMEM((2 * CAP, 128), F32),
            pltpu.VMEM((2 * CAP, 128), F32),
            pltpu.VMEM((PLANE, HALF), BF16),
            pltpu.VMEM((2, PLANE, HALF), BF16),
            pltpu.VMEM((PLANE, HALF), F32),
            pltpu.VMEM((2, 3, 4, ROWS, HALF), BF16),
            pltpu.VMEM((4, 2, 4, ROWS, HALF), BF16),
            pltpu.VMEM((4, 4, ROWS, HALF), BF16),
            pltpu.VMEM((2, 4, ROWS, HALF), F32),
            pltpu.VMEM((2, 3, ROWS, HALF), BF16),
            pltpu.VMEM((4, 3, ROWS, HALF), BF16),
            pltpu.VMEM((3, ROWS, HALF), BF16),
            pltpu.VMEM((3, ROWS, HALF), BF16),
            pltpu.VMEM((2, ROWS, HALF), F32),
            pltpu.VMEM((ROWS, HALF), F32),
            pltpu.VMEM((2, ROWS, HALF), F32),
            pltpu.VMEM((2, 2 * CAP, BLK), BF16),
            DMA((2,)), DMA((2,)), DMA((1,)), DMA((1,)), DMA((3,)), DMA((3,)), DMA((4, 3)), DMA((4, 3)),
            DMA((4, 3, 4)), DMA((4, 3, 4)), DMA((4,)), DMA((4,)), DMA((1,)), DMA((1,)),
            DMA((1,)), DMA((2,)), pltpu.SemaphoreType.REGULAR, DMA((4, 3)), DMA((4, 3)),
            DMA((4, 3, 4)), DMA((4, 3, 4)), DMA((3,)), DMA((3,)), DMA((1,)), DMA((1,)), DMA((1,)), DMA((1,)),
            DMA((2,)), DMA((2,)),
        ],
        compiler_params=pltpu.CompilerParams(collective_id=1, has_side_effects=True, vmem_limit_bytes=61 * 2**20),
        name="gather_and_reduce",
    )(weight, owner, gate.reshape(8, 128), tokens, cotangent)
    grad_gate, grad_tokens, activated, grad_weight = pl.pallas_call(
        combine_kernel,
        out_shape=(
            shape((8, 128), BF16),
            shape((TOK, D), BF16),
            shape((1, 2 * CAP, F), BF16),
            shape((1, 56, F), F32),
        ),
        in_specs=[VMEM, VMEM, ANY, ANY, ANY, ANY],
        out_specs=(VMEM, ANY, ANY, ANY),
        scratch_shapes=[
            pltpu.VMEM((2 * CAP, TOK), BF16),
            pltpu.VMEM((2, 2 * CAP, BLK), BF16),
            pltpu.VMEM((2, TOK, BLK), BF16),
            pltpu.VMEM((TOK, EARLY * BLK), BF16),
            pltpu.VMEM((1, 2 * CAP, F), BF16),
            pltpu.VMEM((1, 56, F), F32),
            DMA((2, 2)), DMA((2,)), DMA((3,)), DMA((3,)),
        ],
        compiler_params=pltpu.CompilerParams(vmem_limit_bytes=60 * 2**20),
        name="combine_tokens",
    )(owner, grad_gate, sg, tok, act, grad_weight)
    return activated, grad_tokens, grad_gate.reshape(TOK), grad_weight


def solution(mesh):
    placed = (
        P(("dp", "expert"), None),
        P(("dp", "expert"), None),
        P(("dp", "expert")),
        P("expert", "dp", None),
        P("expert", "dp", None),
    )
    return jax.shard_map(
        body,
        mesh=mesh,
        in_specs=placed,
        out_specs=(
            P("expert", "dp", None),
            P(("dp", "expert"), None),
            P(("dp", "expert")),
            P("expert", "dp", None),
        ),
        check_vma=False,
    )
```

```python
import jax
import jax.numpy as jnp
from jax import lax
from jax.experimental import pallas as pl
from jax.experimental.pallas import tpu as pltpu
from jax.sharding import PartitionSpec as P

CAP = 640
TOK = 1024
D = 3584
F = 1024
HALF = 512
ROWS = 112
PLANE = 1792
BLK = 512
NBLK = D // BLK
EARLY = 3
MESH = pl.DeviceIdType.MESH
F32 = jnp.float32
BF16 = jnp.bfloat16


def place():
    d, e = lax.axis_index("dp"), lax.axis_index("expert")
    core, z, y, x_lo = d % 2, (d // 2) % 4, (d // 8) % 4, d // 32
    a = y + core * (z - y)
    b = z + core * (y - z)
    return e, x_lo, a, b, core


def device(x, a, b, core):
    x, a, b = x % 4, a % 4, b % 4
    y = a + core * (b - a)
    z = b + core * (a - b)
    return (((x % 2) * 4 + y) * 4 + z) * 2 + core, x // 2


def rows_at(start, size, by=16):
    return pl.ds(pl.multiple_of(start, by), size)


def copy_to(src, dst, send_sem, recv_sem, to):
    return pltpu.make_async_remote_copy(
        src_ref=src, dst_ref=dst, send_sem=send_sem, recv_sem=recv_sem, device_id=to, device_id_type=MESH
    )


def send(*args):
    copy_to(*args).start()


def arrived(ref, sem):
    pltpu.make_async_copy(ref, ref, sem).wait()


def nn(p, q):
    return jnp.dot(p, q, preferred_element_type=F32)


def nt(p, q):
    return lax.dot_general(p, q, (((1,), (1,)), ((), ())), preferred_element_type=F32)


def tn(p, q):
    return lax.dot_general(p, q, (((0,), (0,)), ((), ())), preferred_element_type=F32)


def loop(first, last, f):
    def one(i, carry):
        f(i)
        return carry

    lax.fori_loop(first, last, one, 0)


def one_hot_rows(owner_ref, Q):
    owner = jnp.broadcast_to(owner_ref[...], (8, TOK)).astype(F32)
    upper = (
        lax.broadcasted_iota(jnp.int32, (TOK, TOK), 0) <= lax.broadcasted_iota(jnp.int32, (TOK, TOK), 1)
    ).astype(BF16)
    ones = nn(owner.astype(BF16), upper)
    token = lax.broadcasted_iota(jnp.int32, (8, TOK), 1).astype(F32)
    slot = jnp.where(owner > 0.5, CAP + ones - 1.0, token - ones)[:1].astype(jnp.int32)

    def some(i):
        rows = lax.broadcasted_iota(jnp.int32, (64, TOK), 0) + i * 64
        Q[rows_at(i * 64, 64), :] = (rows == slot).astype(F32).astype(BF16)

    loop(0, 2 * CAP // 64, some)


def main_kernel(
    w_ref, owner_ref, gate_ref, x_hbm, cot_hbm,
    act_out, tok_out, sg_out, gate_out, wg_out,
    W, XS, Q, pre, PG, ACT, ggs, gs,
    SB, RSB, OWN, S, RB, T2, KB, SA, RA, SX, RX, KA, FIN, SG,
    s_loc, s_blk, s_first, r_first, s_x, r_x, s_a, r_a, s_b, r_b, r_far, s_sib, r_sib, s_cot, r_cot,
    s_sb, r_sb, credit, s_ra, r_ra, s_rb, r_rb, r_t2, s_rx, r_rx, s_fin, r_fin, s_act, r_act, s_sg, s_cmb, s_tok,
):
    e, xl, a, b, core = place()
    x = 2 * e + xl
    half = pl.ds(pl.multiple_of(core * HALF, HALF), HALF)
    other = pl.ds(pl.multiple_of((1 - core) * HALF, HALF), HALF)
    sib = device(x, b, a, 1 - core)
    along_x = {o: device(x + o, a, b, core) for o in (1, 2, 3)}
    along_a = {o: device(x, a + o, b, core) for o in (1, 3)}
    along_b = {o: device(x, a, b + o, core) for o in (1, 3)}
    next_a = {o: (a + o) % 4 for o in (1, 2, 3)} | {0: a}
    next_b = {o: (b + o) % 4 for o in (1, 2, 3)} | {0: b}
    step_a, step_b = (4 - 3 * core) * ROWS, (1 + 3 * core) * ROWS
    row_b = {o: next_b[o] * step_b for o in (0, 1, 2, 3)}
    lower, upper = pl.ds(0, 2), pl.ds(2, 2)

    def plane(j):
        ee = e + (j // 2) * (1 - 2 * e)
        flip = ((j + 1) // 2) % 2
        return ee, xl + flip * (1 - 2 * xl)

    def target(j):
        return plane(j + 1 - 2 * (j % 2))

    def away(p):
        return (2 * p[0] + p[1] - x + 4) % 4

    def block_cols(c):
        return pl.ds(pl.multiple_of(c * BLK, BLK), BLK)

    def block_of(i):
        return (i + 3 * xl) % NBLK

    def load_x(i):
        return pltpu.make_async_copy(x_hbm.at[:, block_cols(block_of(i))], SG.at[i % 2, :TOK], s_blk.at[i % 2])

    load_x(0).start()
    load_x(1).start()
    load_cot = pltpu.make_async_copy(cot_hbm.at[0, rows_at(e * CAP, CAP), :], PG.at[e], s_loc.at[0])
    load_cot.start()

    barrier = pltpu.get_barrier_semaphore()
    peers = [sib, *along_x.values(), *along_a.values(), *along_b.values()]
    for peer in peers:
        pl.semaphore_signal(barrier, inc=1, device_id=peer, device_id_type=MESH)
    pl.semaphore_wait(barrier, len(peers))

    left, right = w_ref[0, :, :HALF].astype(F32), w_ref[0, :, HALF:].astype(F32)
    FIN[1, :56] = jnp.where(core == 0, right, left)
    swap = copy_to(FIN.at[1, :56], FIN.at[0, rows_at(core * 56, 56, 8), :], s_first.at[0], r_first.at[0], sib)
    swap.start()
    FIN[0, rows_at(core * 56, 56, 8), :] = jnp.where(core == 0, left, right)
    swap.wait()

    def piece(j, o):
        ee, ll = plane(j)
        aa = next_a[o] if isinstance(o, int) else (a + o) % 4
        return W.at[core, ee, ll, aa + core * (b - aa), b + core * (aa - b)]

    def some_pieces(n):
        return W.at[0, 0, 0, 0, pl.ds(0, n)]

    W[core, e, xl, a + core * (b - a), b + core * (a - b)] = FIN[0].astype(BF16)
    mine = piece(0, 0)

    def send_a(j):
        ref = piece(j, 0)
        for s in (1, 3):
            send(ref, ref, s_a.at[j], r_a.at[j, 3 - s], along_a[s])

    def take_a(j):
        for o in (1, 3):
            arrived(some_pieces(1), r_a.at[j, o - 1])

        @pl.when(j % 2 == 0)
        def _():
            send(piece(j, 3), piece(j, 3), s_a.at[j], r_a.at[j, 1], along_a[1])

        @pl.when(j % 2 == 1)
        def _():
            send(piece(j, 1), piece(j, 1), s_a.at[j], r_a.at[j, 1], along_a[3])

    def far_a(j):
        arrived(some_pieces(1), r_a.at[j, 1])

    def send_rows(j, o, part, send_sem, recv_sem, to):
        ee, ll = plane(j)

        @pl.when(core == 0)
        def _():
            ref = W.at[core, ee, ll, part, next_b[o]]
            send(ref, ref, send_sem, recv_sem, to)

        @pl.when(core == 1)
        def _():
            ref = W.at[core, ee, ll, next_b[o], part]
            send(ref, ref, send_sem, recv_sem, to)

    def send_b(j):
        send_rows(j, 0, lower, s_b.at[j], r_b.at[j, 1, 0], along_b[1])
        send_rows(j, 0, upper, s_b.at[j], r_b.at[j, 0, 1], along_b[3])
        send_rows(j, 0, upper, s_b.at[j], r_b.at[j, 1, 1], along_b[1])
        send_rows(j, 0, lower, s_b.at[j], r_b.at[j, 0, 0], along_b[3])

    def relay_b(j):
        arrived(some_pieces(2), r_b.at[j, 1, 0])
        send_rows(j, 3, lower, s_b.at[j], r_far.at[j, 0], along_b[1])
        arrived(some_pieces(2), r_b.at[j, 0, 1])
        send_rows(j, 1, upper, s_b.at[j], r_far.at[j, 1], along_b[3])

    def rest_b(j):
        arrived(some_pieces(2), r_b.at[j, 1, 1])
        arrived(some_pieces(2), r_b.at[j, 0, 0])

    def far_b(j):
        for i in (0, 1):
            arrived(some_pieces(2), r_far.at[j, i])
        ee, ll = plane(j)
        ref = W.at[core, ee, ll]
        send(ref, ref, s_sib.at[j], r_sib.at[j], sib)

    def whole(j):
        ee, ll = plane(j)
        arrived(W.at[1 - core, ee, ll], r_sib.at[j])

    for s in (1, 3, 2):
        send(mine, mine, s_x.at[0], r_x.at[3 - s], along_x[s])
    send_a(0)

    one_hot_rows(owner_ref, Q)
    take_a(0)
    g8 = gate_ref[...].astype(F32)
    gate_row = jnp.concatenate([g8[i : i + 1] for i in range(8)], axis=1)
    gs[...] = nt(Q[...], jnp.broadcast_to(gate_row, (128, TOK)).astype(BF16)).astype(BF16)
    far_a(0)
    send_b(0)

    def dispatch(i):
        load_x(i).wait()
        for m in (0, CAP):
            XS[m : m + CAP, block_cols(block_of(i))] = nn(Q[m : m + CAP, :], SG[i % 2, :TOK]).astype(BF16)

        @pl.when(i < NBLK - 2)
        def _():
            load_x(i + 2).start()

    def start_a(j):
        arrived(some_pieces(1), r_x.at[away(plane(j)) - 1])
        send_a(j)

    loop(1, 4, start_a)
    dispatch(0)
    loop(1, 4, take_a)
    theirs_rows = rows_at((1 - e) * CAP, CAP)
    send(cot_hbm.at[0, theirs_rows, :], PG.at[e], s_cot.at[0], r_cot.at[0], along_x[2])
    far_a(1)
    send_b(1)
    dispatch(1)

    def forward(j, h):
        ee, ll = plane(j)
        cols = slice(h * HALF, (h + 1) * HALF)

        def some(i):
            rows = rows_at(i * 320, 320, 64)
            slots = XS[rows_at(ee * CAP + i * 320, 320, 64), pl.ds(pl.multiple_of(ll * PLANE, 256), PLANE)]
            part = nn(slots, W[h, ee, ll].reshape(PLANE, HALF))
            pre[rows, cols] = jnp.where(j % 2 == 0, part, pre[rows, cols] + part)

        loop(0, 2, some)

    def pointwise(k):
        def tile(i):
            rows = rows_at(i * 64, 64, 64)
            gate = gs[rows_at(k * CAP + i * 64, 64, 64), :].astype(F32)
            gate = jnp.concatenate([gate] * 4, axis=1)
            total = jnp.zeros((64, 1), F32)
            for h in (0, 1):
                cols = slice(h * HALF, (h + 1) * HALF)
                z = pre[rows, cols]
                s = 0.5 + 0.5 * jnp.tanh(0.5 * z)
                shaped = z * s
                up = PG[k, rows, cols].astype(F32)
                ACT[rows, cols] = (gate * shaped).astype(BF16)
                total += jnp.sum(up * shaped, axis=1, keepdims=True)
                PG[k, rows, cols] = (up * gate * (s * (1.0 + z * (1.0 - s)))).astype(BF16)
            ggs[rows_at(k * CAP + i * 64, 64, 64), :] = jnp.broadcast_to(total, (64, 128)).astype(BF16)

        loop(0, CAP // 64, tile)

    def theirs(j):
        ee, ll = target(j)
        def some(i):
            part = XS[rows_at(ee * CAP, CAP), pl.ds(pl.multiple_of(ll * PLANE + i * 896, 128), 896)]
            SB[rows_at(i * 896, 896, 128), :] = tn(part, PG[ee, :, other]).astype(BF16)

        loop(0, 2, some)
        send(SB, RSB.at[j % 2], s_sb.at[0], r_sb.at[j % 2], sib)

    def ours(j):
        ee, ll = target(j)
        def some(i):
            part = XS[rows_at(ee * CAP, CAP), pl.ds(pl.multiple_of(ll * PLANE + i * 896, 128), 896)]
            OWN[rows_at(i * 896, 896, 128), :] = tn(part, PG[ee, :, half])

        loop(0, 2, some)

    def first_sends(j):
        arrived(RSB.at[j % 2], r_sb.at[j % 2])
        k = j % 2

        def summed(i, o):
            rows = rows_at(row_b[o] + i * step_a, ROWS)
            return rows, OWN[rows, :] + RSB[k, rows, :].astype(F32)

        def put(o, part, dst, sem, to):
            for i in part:
                S[k, o - 1, i] = summed(i, o)[1].astype(BF16)
            part = lower if part[0] == 0 else upper
            send(S.at[k, o - 1, part], dst.at[part], s_rb.at[j], sem, to)

        put(2, (0, 1), T2.at[j], r_t2.at[j, 0], along_b[1])
        put(2, (2, 3), T2.at[j], r_t2.at[j, 1], along_b[3])
        put(1, (2, 3), RB.at[j, 1], r_rb.at[j, 1, 1], along_b[1])
        put(3, (0, 1), RB.at[j, 0], r_rb.at[j, 0, 0], along_b[3])
        for i in (0, 1, 2, 3):
            KB[k, i] = summed(i, 0)[1]
            rows, total = summed(i, 1 if i < 2 else 3)
            OWN[rows, :] = total

    def relayed_sends(j):
        k = j % 2
        for n, (part, o) in enumerate(((lower, 1), (upper, 3))):
            arrived(T2.at[j, part], r_t2.at[j, n])
            for i in (2 * n, 2 * n + 1):
                rows = rows_at(row_b[o] + i * step_a, ROWS)
                S[k, o - 1, i] = (OWN[rows, :] + T2[j, i].astype(F32)).astype(BF16)
            d = 1 - n
            send(S.at[k, o - 1, part], RB.at[j, d, part], s_rb.at[j], r_rb.at[j, d, n], along_b[o])

    def sent_b(j):
        arrived(S.at[j % 2], s_rb.at[j])

    def sent_a(j):
        arrived(SA.at[j % 2], s_ra.at[j])

    def finish_b(j):
        k = j % 2
        for d in (0, 1):
            for n, part in enumerate((lower, upper)):
                arrived(RB.at[j, d, part], r_rb.at[j, d, n])

        def total(o):
            i = next_a[o]
            return KB[k, i] + RB[j, 0, i].astype(F32) + RB[j, 1, i].astype(F32)

        @pl.when(j >= 2)
        def _():
            sent_a(j - 2)

        KA[k] = total(0)
        SA[k, 1] = total(2).astype(BF16)
        keep, go = total(1), total(3)

        @pl.when(k == 0)
        def _():
            send(SA.at[k, 1], RA.at[j, 1], s_ra.at[j], r_ra.at[j, 1], along_a[1])
            SA[k, 2] = go.astype(BF16)
            send(SA.at[k, 2], RA.at[j, 0], s_ra.at[j], r_ra.at[j, 0], along_a[3])
            FIN[1] = keep

        @pl.when(k == 1)
        def _():
            send(SA.at[k, 1], RA.at[j, 1], s_ra.at[j], r_ra.at[j, 1], along_a[3])
            SA[k, 0] = keep.astype(BF16)
            send(SA.at[k, 0], RA.at[j, 2], s_ra.at[j], r_ra.at[j, 2], along_a[1])
            FIN[1] = go

    def relay_a(j):
        k = j % 2
        arrived(RA.at[j, 1], r_ra.at[j, 1])

        @pl.when(k == 0)
        def _():
            SA[k, 0] = (FIN[1] + RA[j, 1].astype(F32)).astype(BF16)
            send(SA.at[k, 0], RA.at[j, 2], s_ra.at[j], r_ra.at[j, 2], along_a[1])

        @pl.when(k == 1)
        def _():
            SA[k, 2] = (FIN[1] + RA[j, 1].astype(F32)).astype(BF16)
            send(SA.at[k, 2], RA.at[j, 0], s_ra.at[j], r_ra.at[j, 0], along_a[3])

    def finish_a(j):
        total = KA[j % 2]
        for o in (1, 3):
            arrived(RA.at[j, o - 1], r_ra.at[j, o - 1])
            total += RA[j, o - 1].astype(F32)
        return total

    def finish_x(j):
        o = away(target(j))
        SX[o - 1] = finish_a(j).astype(BF16)
        send(SX.at[o - 1], RX.at[3 - o], s_rx.at[0], r_rx.at[3 - o], device(x + o, a, b, core))

    def slot_grad(q):
        k, n = e + (q // 4) * (1 - 2 * e), q % 4
        some = pl.ds((n % 2) * 2, 2)
        slot = q % 2

        @pl.when(q >= 2)
        def _():
            sent_sg(slot)

        def half_rows(i):
            m = rows_at(i * 320, 320, 64)
            near, far = (W[h, k, n // 2, some].reshape(896, HALF) for h in (0, 1))
            part = (nt(PG[k, m, :HALF], near) + nt(PG[k, m, HALF:], far)).astype(BF16)
            SG[0, rows_at(slot * CAP + i * 320, 320, 64), :] = part[:, :BLK]
            SG[1, rows_at(slot * CAP + i * 320, 320, 64), :384] = part[:, BLK:]

        loop(0, 2, half_rows)
        rows = rows_at(slot * CAP, CAP, 64)
        for i, (at, width) in enumerate(((0, BLK), (BLK, 384))):
            cols = pl.ds(pl.multiple_of(n * 896 + at, 128), width)
            pltpu.make_async_copy(SG.at[i, rows, :width], sg_out.at[k, :, cols], s_sg.at[slot, i]).start()

    def sent_sg(slot):
        arrived(SG.at[0, :CAP, :], s_sg.at[slot, 0])
        arrived(SG.at[1, :CAP, :384], s_sg.at[slot, 1])

    def slot_grads(first, last):
        loop(first, last, slot_grad)

    def gather_step(j):
        @pl.when(j == 3)
        def _():
            first_sends(0)
            pl.semaphore_signal(credit, inc=1, device_id=sib, device_id_type=MESH)

        relay_b(j)

        @pl.when(j == 0)
        def _():
            loop(2, 4, dispatch)

        @pl.when(j > 0)
        def _():
            whole(j - 1)
            forward(j - 1, 0)

        rest_b(j)

        @pl.when(j < 2)
        def _():
            far_a(j + 2)
            send_b(j + 2)

        @pl.when(j == 0)
        def _():
            dispatch(4)

        @pl.when(j > 0)
        def _():
            forward(j - 1, 1)

        @pl.when(j == 1)
        def _():
            loop(5, NBLK, dispatch)

        @pl.when(j == 2)
        def _():
            load_cot.wait()
            pointwise(e)
            theirs(0)
            pltpu.make_async_copy(ACT, act_out.at[0, rows_at(e * CAP, CAP), :], s_loc.at[1]).start()

        @pl.when(j == 3)
        def _():
            arrived(SB, s_sb.at[0])
            theirs(1)

        far_b(j)

        @pl.when(j == 2)
        def _():
            ours(0)

    loop(0, 4, gather_step)

    def reduce_step(j):
        @pl.when(j == 0)
        def _():
            slot_grads(0, 1)

        relayed_sends(j)

        @pl.when(j < 3)
        def _():
            ours(j + 1)

            @pl.when(j >= 1)
            def _():
                sent_b(j - 1)

            first_sends(j + 1)

        @pl.when(j == 0)
        def _():
            pl.semaphore_signal(credit, inc=1, device_id=sib, device_id_type=MESH)
            whole(3)
            forward(3, 0)
            forward(3, 1)
            arrived(PG.at[1 - e], r_cot.at[0])
            arrived(ACT, s_loc.at[1])
            pointwise(1 - e)
            send(ACT, act_out.at[0, rows_at(e * CAP, CAP), :], s_act.at[0], r_act.at[0], along_x[2])

        @pl.when(j < 2)
        def _():
            arrived(SB, s_sb.at[0])
            pl.semaphore_wait(credit, 1)
            theirs(j + 2)

        @pl.when(j >= 1)
        def _():
            relay_a(j - 1)

        @pl.when(j == 2)
        def _():
            finish_x(0)

        @pl.when(j == 3)
        def _():
            FIN[0] = finish_a(1)

        @pl.when(j >= 1)
        def _():
            slot_grads(2 * j, 2 * j + 2)

        @pl.when(j == 0)
        def _():
            slot_grads(1, 2)

        finish_b(j)

    loop(0, 4, reduce_step)
    sent_sg(0)
    sent_sg(1)

    def early(c):
        for k in (0, 1):
            pltpu.make_async_copy(
                sg_out.at[k, :, block_cols(c)], SG.at[c % 2, k * CAP : (k + 1) * CAP], s_cmb.at[c % 2]
            ).start()

    def combine(c):
        arrived(SG.at[c % 2], s_cmb.at[c % 2])

        @pl.when(c >= 2)
        def _():
            arrived(RSB.at[c % 2, :TOK], s_tok.at[c % 2])

        def some(i):
            m = pl.ds(pl.multiple_of(i * 512, 512), 512)
            RSB[c % 2, m] = tn(Q[:, m], SG[c % 2]).astype(BF16)

        loop(0, 2, some)
        pltpu.make_async_copy(RSB.at[c % 2, :TOK], tok_out.at[:, block_cols(c)], s_tok.at[c % 2]).start()

        @pl.when(c + 2 < EARLY)
        def _():
            early(c + 2)

    early(0)
    early(1)
    finish_x(2)
    combine(0)
    relay_a(3)
    loop(1, EARLY, combine)
    gg = ggs[...].astype(F32).T[:8].astype(BF16)
    row = nn(gg, Q[...])
    gate_out[...] = jnp.concatenate([row[:1, i * 128 : (i + 1) * 128] for i in range(8)], axis=0)
    finish_x(3)
    total = FIN[0]
    for o in (1, 2, 3):
        arrived(RX.at[o - 1], r_rx.at[o - 1])
        total += RX[o - 1].astype(F32)
    FIN[0] = total
    away_rows = rows_at((1 - core) * 56, 56, 8)
    kept_rows = rows_at(core * 56, 56, 8)
    last = copy_to(FIN.at[0, away_rows, :], FIN.at[2, away_rows, :], s_fin.at[0], r_fin.at[0], sib)
    last.start()
    last.wait_send()
    arrived(FIN.at[2, kept_rows, :], r_fin.at[0])
    kept, came = FIN[0, kept_rows, :], FIN[2, kept_rows, :]
    wg_out[0, :, :HALF] = jnp.where(core == 0, kept, came)
    wg_out[0, :, HALF:] = jnp.where(core == 0, came, kept)

    arrived(some_pieces(3), s_x.at[0])
    arrived(SX, s_rx.at[0])
    arrived(cot_hbm.at[0, theirs_rows, :], s_cot.at[0])
    arrived(ACT, s_act.at[0])
    arrived(SB, s_sb.at[0])
    arrived(act_out.at[0, theirs_rows, :], r_act.at[0])
    for i in (0, 1):
        arrived(RSB.at[i, :TOK], s_tok.at[i])

    def drain(j):
        arrived(some_pieces(3), s_a.at[j])
        arrived(W.at[0, 0, 0, pl.ds(0, 3)], s_b.at[j])
        arrived(W.at[0, 0, 0], s_sib.at[j])

        @pl.when(j >= 2)
        def _():
            sent_a(j)
            sent_b(j)

    loop(0, 4, drain)


def combine_kernel(
    owner_ref, gate_ref, sg_hbm, tok_hbm, act_hbm, wg_hbm,
    gate_out, tok_out, act_out, wg_out,
    Q, SG, TB, TV, AV, GV, s_sg, s_tok, s_in, s_out,
):
    def cols(c):
        return pl.ds(pl.multiple_of(c * BLK, BLK), BLK)

    def load(c):
        return [
            pltpu.make_async_copy(
                sg_hbm.at[k, :, cols(c)], SG.at[c % 2, k * CAP : (k + 1) * CAP], s_sg.at[c % 2, k]
            )
            for k in (0, 1)
        ]

    moves = [
        (act_hbm, AV, act_out),
        (tok_hbm, TV, tok_out.at[:, : EARLY * BLK]),
        (wg_hbm, GV, wg_out),
    ]
    moves = [
        (pltpu.make_async_copy(p, v, s_in.at[i]), pltpu.make_async_copy(v, q, s_out.at[i]))
        for i, (p, v, q) in enumerate(moves)
    ]
    for c in (EARLY, EARLY + 1):
        for k in load(c):
            k.start()
    for k, _ in moves:
        k.start()
    one_hot_rows(owner_ref, Q)
    gate_out[...] = gate_ref[...].astype(BF16)

    def combine(c):
        for k in load(c):
            k.wait()

        @pl.when(c >= EARLY + 2)
        def _():
            arrived(TB.at[c % 2], s_tok.at[c % 2])

        TB[c % 2] = tn(Q[...], SG[c % 2]).astype(BF16)
        pltpu.make_async_copy(TB.at[c % 2], tok_out.at[:, cols(c)], s_tok.at[c % 2]).start()

        @pl.when(c + 2 < NBLK)
        def _():
            for k in load(c + 2):
                k.start()

    loop(EARLY, EARLY + 1, combine)
    for k, m in moves:
        k.wait()
        m.start()
    loop(EARLY + 1, NBLK, combine)
    for i in (0, 1):
        arrived(TB.at[i], s_tok.at[i])
    for _, m in moves:
        m.wait()


def body(tokens, assignment, gate, weight, cotangent):
    ANY, VMEM = pl.BlockSpec(memory_space=pl.ANY), pl.BlockSpec(memory_space=pltpu.VMEM)
    DMA = pltpu.SemaphoreType.DMA
    shape = jax.ShapeDtypeStruct
    owner = assignment.reshape(1, TOK)
    act, tok, sg, grad_gate, grad_weight = pl.pallas_call(
        main_kernel,
        out_shape=(
            shape((1, 2 * CAP, F), BF16),
            shape((TOK, EARLY * BLK), BF16),
            shape((2, CAP, D), BF16),
            shape((8, 128), F32),
            shape((1, 56, F), F32),
        ),
        in_specs=[VMEM, VMEM, VMEM, ANY, ANY],
        out_specs=(ANY, ANY, ANY, VMEM, VMEM),
        scratch_shapes=[
            pltpu.VMEM((2, 2, 2, 4, 4, ROWS, HALF), BF16),
            pltpu.VMEM((2 * CAP, D), BF16),
            pltpu.VMEM((2 * CAP, TOK), BF16),
            pltpu.VMEM((CAP, F), F32),
            pltpu.VMEM((2, CAP, F), BF16),
            pltpu.VMEM((CAP, F), BF16),
            pltpu.VMEM((2 * CAP, 128), BF16),
            pltpu.VMEM((2 * CAP, 128), BF16),
            pltpu.VMEM((PLANE, HALF), BF16),
            pltpu.VMEM((2, PLANE, HALF), BF16),
            pltpu.VMEM((PLANE, HALF), F32),
            pltpu.VMEM((2, 3, 4, ROWS, HALF), BF16),
            pltpu.VMEM((4, 2, 4, ROWS, HALF), BF16),
            pltpu.VMEM((4, 4, ROWS, HALF), BF16),
            pltpu.VMEM((2, 4, ROWS, HALF), F32),
            pltpu.VMEM((2, 3, ROWS, HALF), BF16),
            pltpu.VMEM((4, 3, ROWS, HALF), BF16),
            pltpu.VMEM((3, ROWS, HALF), BF16),
            pltpu.VMEM((3, ROWS, HALF), BF16),
            pltpu.VMEM((2, ROWS, HALF), F32),
            pltpu.VMEM((3, ROWS, HALF), F32),
            pltpu.VMEM((2, 2 * CAP, BLK), BF16),
            DMA((2,)), DMA((2,)), DMA((1,)), DMA((1,)), DMA((1,)), DMA((3,)), DMA((4,)), DMA((4, 3)),
            DMA((4,)), DMA((4, 2, 2)), DMA((4, 2)), DMA((4,)), DMA((4,)), DMA((1,)), DMA((1,)),
            DMA((1,)), DMA((2,)), pltpu.SemaphoreType.REGULAR, DMA((4,)), DMA((4, 3)),
            DMA((4,)), DMA((4, 2, 2)), DMA((4, 2)), DMA((1,)), DMA((3,)), DMA((1,)), DMA((1,)), DMA((1,)), DMA((1,)),
            DMA((2, 2)), DMA((2,)), DMA((2,)),
        ],
        compiler_params=pltpu.CompilerParams(collective_id=1, has_side_effects=True, vmem_limit_bytes=62 * 2**20),
        name="gather_and_reduce",
    )(weight, owner, gate.reshape(8, 128), tokens, cotangent)
    grad_gate, grad_tokens, activated, grad_weight = pl.pallas_call(
        combine_kernel,
        out_shape=(
            shape((8, 128), BF16),
            shape((TOK, D), BF16),
            shape((1, 2 * CAP, F), BF16),
            shape((1, 56, F), F32),
        ),
        in_specs=[VMEM, VMEM, ANY, ANY, ANY, ANY],
        out_specs=(VMEM, ANY, ANY, ANY),
        scratch_shapes=[
            pltpu.VMEM((2 * CAP, TOK), BF16),
            pltpu.VMEM((2, 2 * CAP, BLK), BF16),
            pltpu.VMEM((2, TOK, BLK), BF16),
            pltpu.VMEM((TOK, EARLY * BLK), BF16),
            pltpu.VMEM((1, 2 * CAP, F), BF16),
            pltpu.VMEM((1, 56, F), F32),
            DMA((2, 2)), DMA((2,)), DMA((3,)), DMA((3,)),
        ],
        compiler_params=pltpu.CompilerParams(vmem_limit_bytes=60 * 2**20),
        name="combine_tokens",
    )(owner, grad_gate, sg, tok, act, grad_weight)
    return activated, grad_tokens, grad_gate.reshape(TOK), grad_weight


def solution(mesh):
    placed = (
        P(("dp", "expert"), None),
        P(("dp", "expert"), None),
        P(("dp", "expert")),
        P("expert", "dp", None),
        P("expert", "dp", None),
    )
    return jax.shard_map(
        body,
        mesh=mesh,
        in_specs=placed,
        out_specs=(
            P("expert", "dp", None),
            P(("dp", "expert"), None),
            P(("dp", "expert")),
            P("expert", "dp", None),
        ),
        check_vma=False,
    )
```

```python
import jax
import jax.numpy as jnp
from jax import lax
from jax.experimental import pallas as pl
from jax.experimental.pallas import tpu as pltpu
from jax.sharding import PartitionSpec as P

CAP = 640
TOK = 1024
D = 3584
F = 1024
HALF = 512
ROWS = 112
PLANE = 1792
BLK = 512
NBLK = D // BLK
EARLY = 3
MESH = pl.DeviceIdType.MESH
F32 = jnp.float32
BF16 = jnp.bfloat16


def place():
    d, e = lax.axis_index("dp"), lax.axis_index("expert")
    core, z, y, x_lo = d % 2, (d // 2) % 4, (d // 8) % 4, d // 32
    a = y + core * (z - y)
    b = z + core * (y - z)
    return e, x_lo, a, b, core


def device(x, a, b, core):
    x, a, b = x % 4, a % 4, b % 4
    y = a + core * (b - a)
    z = b + core * (a - b)
    return (((x % 2) * 4 + y) * 4 + z) * 2 + core, x // 2


def rows_at(start, size, by=16):
    return pl.ds(pl.multiple_of(start, by), size)


def copy_to(src, dst, send_sem, recv_sem, to):
    return pltpu.make_async_remote_copy(
        src_ref=src, dst_ref=dst, send_sem=send_sem, recv_sem=recv_sem, device_id=to, device_id_type=MESH
    )


def send(*args):
    copy_to(*args).start()


def arrived(ref, sem):
    pltpu.make_async_copy(ref, ref, sem).wait()


def nn(p, q):
    return jnp.dot(p, q, preferred_element_type=F32)


def nt(p, q):
    return lax.dot_general(p, q, (((1,), (1,)), ((), ())), preferred_element_type=F32)


def tn(p, q):
    return lax.dot_general(p, q, (((0,), (0,)), ((), ())), preferred_element_type=F32)


def loop(first, last, f):
    def one(i, carry):
        f(i)
        return carry

    lax.fori_loop(first, last, one, 0)


def one_hot_rows(owner_ref, Q):
    owner = jnp.broadcast_to(owner_ref[...], (8, TOK)).astype(F32)
    upper = (
        lax.broadcasted_iota(jnp.int32, (TOK, TOK), 0) <= lax.broadcasted_iota(jnp.int32, (TOK, TOK), 1)
    ).astype(BF16)
    ones = nn(owner.astype(BF16), upper)
    token = lax.broadcasted_iota(jnp.int32, (8, TOK), 1).astype(F32)
    slot = jnp.where(owner > 0.5, CAP + ones - 1.0, token - ones)[:1].astype(jnp.int32)

    def some(i):
        rows = lax.broadcasted_iota(jnp.int32, (64, TOK), 0) + i * 64
        Q[rows_at(i * 64, 64), :] = (rows == slot).astype(F32).astype(BF16)

    loop(0, 2 * CAP // 64, some)


def main_kernel(
    w_ref, owner_ref, gate_ref, x_hbm, cot_hbm,
    act_out, tok_out, sg_out, gate_out, wg_out,
    W, XS, Q, pre, PG, ACT, ggs, gs,
    SB, RSB, OWN, S, RB, T2, KB, SA, RA, SX, RX, KA, FIN, SG,
    s_loc, s_blk, s_first, r_first, s_x, r_x, s_a, r_a, s_b, r_b, r_far, s_sib, r_sib, s_cot, r_cot,
    s_sb, r_sb, credit, s_ra, r_ra, s_rb, r_rb, r_t2, s_rx, r_rx, s_fin, r_fin, s_act, r_act, s_sg, s_cmb, s_tok,
):
    e, xl, a, b, core = place()
    x = 2 * e + xl
    half = pl.ds(pl.multiple_of(core * HALF, HALF), HALF)
    other = pl.ds(pl.multiple_of((1 - core) * HALF, HALF), HALF)
    sib = device(x, b, a, 1 - core)
    along_x = {o: device(x + o, a, b, core) for o in (1, 2, 3)}
    along_a = {o: device(x, a + o, b, core) for o in (1, 3)}
    along_b = {o: device(x, a, b + o, core) for o in (1, 3)}
    next_a = {o: (a + o) % 4 for o in (1, 2, 3)} | {0: a}
    next_b = {o: (b + o) % 4 for o in (1, 2, 3)} | {0: b}
    step_a, step_b = (4 - 3 * core) * ROWS, (1 + 3 * core) * ROWS
    row_b = {o: next_b[o] * step_b for o in (0, 1, 2, 3)}
    lower, upper = pl.ds(0, 2), pl.ds(2, 2)

    def plane(j):
        ee = e + (j // 2) * (1 - 2 * e)
        flip = ((j + 1) // 2) % 2
        return ee, xl + flip * (1 - 2 * xl)

    def target(j):
        return plane(j + 1 - 2 * (j % 2))

    def away(p):
        return (2 * p[0] + p[1] - x + 4) % 4

    def block_cols(c):
        return pl.ds(pl.multiple_of(c * BLK, BLK), BLK)

    def block_of(i):
        return (i + 3 * xl) % NBLK

    def load_x(i):
        return pltpu.make_async_copy(x_hbm.at[:, block_cols(block_of(i))], SG.at[i % 2, :TOK], s_blk.at[i % 2])

    load_x(0).start()
    load_x(1).start()
    load_cot = pltpu.make_async_copy(cot_hbm.at[0, rows_at(e * CAP, CAP), :], PG.at[e], s_loc.at[0])
    load_cot.start()

    barrier = pltpu.get_barrier_semaphore()
    peers = [sib, *along_x.values(), *along_a.values(), *along_b.values()]
    for peer in peers:
        pl.semaphore_signal(barrier, inc=1, device_id=peer, device_id_type=MESH)
    pl.semaphore_wait(barrier, len(peers))

    left, right = w_ref[0, :, :HALF].astype(F32), w_ref[0, :, HALF:].astype(F32)
    FIN[1, :56] = jnp.where(core == 0, right, left)
    swap = copy_to(FIN.at[1, :56], FIN.at[0, rows_at(core * 56, 56, 8), :], s_first.at[0], r_first.at[0], sib)
    swap.start()
    FIN[0, rows_at(core * 56, 56, 8), :] = jnp.where(core == 0, left, right)
    swap.wait()

    def piece(j, o):
        ee, ll = plane(j)
        aa = next_a[o] if isinstance(o, int) else (a + o) % 4
        return W.at[core, ee, ll, aa + core * (b - aa), b + core * (aa - b)]

    def some_pieces(n):
        return W.at[0, 0, 0, 0, pl.ds(0, n)]

    W[core, e, xl, a + core * (b - a), b + core * (a - b)] = FIN[0].astype(BF16)
    mine = piece(0, 0)

    def send_a(j):
        ref = piece(j, 0)
        for s in (1, 3):
            send(ref, ref, s_a.at[j], r_a.at[j, 3 - s], along_a[s])

    def take_a(j):
        for o in (1, 3):
            arrived(some_pieces(1), r_a.at[j, o - 1])

        @pl.when(j % 2 == 0)
        def _():
            send(piece(j, 3), piece(j, 3), s_a.at[j], r_a.at[j, 1], along_a[1])

        @pl.when(j % 2 == 1)
        def _():
            send(piece(j, 1), piece(j, 1), s_a.at[j], r_a.at[j, 1], along_a[3])

    def far_a(j):
        arrived(some_pieces(1), r_a.at[j, 1])

    def send_rows(j, o, part, send_sem, recv_sem, to):
        ee, ll = plane(j)

        @pl.when(core == 0)
        def _():
            ref = W.at[core, ee, ll, part, next_b[o]]
            send(ref, ref, send_sem, recv_sem, to)

        @pl.when(core == 1)
        def _():
            ref = W.at[core, ee, ll, next_b[o], part]
            send(ref, ref, send_sem, recv_sem, to)

    def send_b(j):
        send_rows(j, 0, lower, s_b.at[j], r_b.at[j, 1, 0], along_b[1])
        send_rows(j, 0, upper, s_b.at[j], r_b.at[j, 0, 1], along_b[3])
        send_rows(j, 0, upper, s_b.at[j], r_b.at[j, 1, 1], along_b[1])
        send_rows(j, 0, lower, s_b.at[j], r_b.at[j, 0, 0], along_b[3])

    def relay_b(j):
        arrived(some_pieces(2), r_b.at[j, 1, 0])
        send_rows(j, 3, lower, s_b.at[j], r_far.at[j, 0], along_b[1])
        arrived(some_pieces(2), r_b.at[j, 0, 1])
        send_rows(j, 1, upper, s_b.at[j], r_far.at[j, 1], along_b[3])

    def rest_b(j):
        arrived(some_pieces(2), r_b.at[j, 1, 1])
        arrived(some_pieces(2), r_b.at[j, 0, 0])

    def far_b(j):
        for i in (0, 1):
            arrived(some_pieces(2), r_far.at[j, i])
        ee, ll = plane(j)
        ref = W.at[core, ee, ll]
        send(ref, ref, s_sib.at[j], r_sib.at[j], sib)

    def whole(j):
        ee, ll = plane(j)
        arrived(W.at[1 - core, ee, ll], r_sib.at[j])

    for s in (1, 3, 2):
        send(mine, mine, s_x.at[0], r_x.at[3 - s], along_x[s])
    send_a(0)

    one_hot_rows(owner_ref, Q)
    take_a(0)
    g8 = gate_ref[...].astype(F32)
    gate_row = jnp.concatenate([g8[i : i + 1] for i in range(8)], axis=1)
    gs[...] = nt(Q[...], jnp.broadcast_to(gate_row, (128, TOK)).astype(BF16)).astype(BF16)
    far_a(0)
    send_b(0)

    def dispatch(i):
        load_x(i).wait()
        for m in (0, CAP):
            XS[m : m + CAP, block_cols(block_of(i))] = nn(Q[m : m + CAP, :], SG[i % 2, :TOK]).astype(BF16)

        @pl.when(i < NBLK - 2)
        def _():
            load_x(i + 2).start()

    def start_a(j):
        arrived(some_pieces(1), r_x.at[away(plane(j)) - 1])
        send_a(j)

    loop(1, 4, start_a)
    dispatch(0)
    loop(1, 4, take_a)
    theirs_rows = rows_at((1 - e) * CAP, CAP)
    send(cot_hbm.at[0, theirs_rows, :], PG.at[e], s_cot.at[0], r_cot.at[0], along_x[2])
    far_a(1)
    send_b(1)
    dispatch(1)

    def forward(j, h):
        ee, ll = plane(j)
        cols = slice(h * HALF, (h + 1) * HALF)
        slots = XS[rows_at(ee * CAP, CAP), pl.ds(pl.multiple_of(ll * PLANE, 256), PLANE)]
        part = nn(slots, W[h, ee, ll].reshape(PLANE, HALF))
        pre[:, cols] = jnp.where(j % 2 == 0, part, pre[:, cols] + part)

    def pointwise(k):
        def tile(i):
            rows = rows_at(i * 64, 64, 64)
            gate = gs[rows_at(k * CAP + i * 64, 64, 64), :].astype(F32)
            gate = jnp.concatenate([gate] * 4, axis=1)
            total = jnp.zeros((64, 1), F32)
            for h in (0, 1):
                cols = slice(h * HALF, (h + 1) * HALF)
                z = pre[rows, cols]
                s = 0.5 + 0.5 * jnp.tanh(0.5 * z)
                shaped = z * s
                up = PG[k, rows, cols].astype(F32)
                ACT[rows, cols] = (gate * shaped).astype(BF16)
                total += jnp.sum(up * shaped, axis=1, keepdims=True)
                PG[k, rows, cols] = (up * gate * (s * (1.0 + z * (1.0 - s)))).astype(BF16)
            ggs[rows_at(k * CAP + i * 64, 64, 64), :] = jnp.broadcast_to(total, (64, 128)).astype(BF16)

        loop(0, CAP // 64, tile)

    def theirs(j):
        ee, ll = target(j)
        def some(i):
            part = XS[rows_at(ee * CAP, CAP), pl.ds(pl.multiple_of(ll * PLANE + i * 896, 128), 896)]
            SB[rows_at(i * 896, 896, 128), :] = tn(part, PG[ee, :, other]).astype(BF16)

        loop(0, 2, some)
        send(SB, RSB.at[j % 2], s_sb.at[0], r_sb.at[j % 2], sib)

    def ours(j):
        ee, ll = target(j)
        def some(i):
            part = XS[rows_at(ee * CAP, CAP), pl.ds(pl.multiple_of(ll * PLANE + i * 896, 128), 896)]
            OWN[rows_at(i * 896, 896, 128), :] = tn(part, PG[ee, :, half])

        loop(0, 2, some)

    def first_sends(j):
        arrived(RSB.at[j % 2], r_sb.at[j % 2])
        k = j % 2

        def summed(i, o):
            rows = rows_at(row_b[o] + i * step_a, ROWS)
            return rows, OWN[rows, :] + RSB[k, rows, :].astype(F32)

        def put(o, part, dst, sem, to):
            for i in part:
                S[k, o - 1, i] = summed(i, o)[1].astype(BF16)
            part = lower if part[0] == 0 else upper
            send(S.at[k, o - 1, part], dst.at[part], s_rb.at[j], sem, to)

        put(2, (0, 1), T2.at[j], r_t2.at[j, 0], along_b[1])
        put(2, (2, 3), T2.at[j], r_t2.at[j, 1], along_b[3])
        put(1, (2, 3), RB.at[j, 1], r_rb.at[j, 1, 1], along_b[1])
        put(3, (0, 1), RB.at[j, 0], r_rb.at[j, 0, 0], along_b[3])
        for i in (0, 1, 2, 3):
            KB[k, i] = summed(i, 0)[1]
            rows, total = summed(i, 1 if i < 2 else 3)
            OWN[rows, :] = total

    def relayed_sends(j):
        k = j % 2
        for n, (part, o) in enumerate(((lower, 1), (upper, 3))):
            arrived(T2.at[j, part], r_t2.at[j, n])
            for i in (2 * n, 2 * n + 1):
                rows = rows_at(row_b[o] + i * step_a, ROWS)
                S[k, o - 1, i] = (OWN[rows, :] + T2[j, i].astype(F32)).astype(BF16)
            d = 1 - n
            send(S.at[k, o - 1, part], RB.at[j, d, part], s_rb.at[j], r_rb.at[j, d, n], along_b[o])

    def sent_b(j):
        arrived(S.at[j % 2], s_rb.at[j])

    def sent_a(j):
        arrived(SA.at[j % 2], s_ra.at[j])

    def finish_b(j):
        k = j % 2
        for d in (0, 1):
            for n, part in enumerate((lower, upper)):
                arrived(RB.at[j, d, part], r_rb.at[j, d, n])

        def total(o):
            i = next_a[o]
            return KB[k, i] + RB[j, 0, i].astype(F32) + RB[j, 1, i].astype(F32)

        @pl.when(j >= 2)
        def _():
            sent_a(j - 2)

        KA[k] = total(0)
        SA[k, 1] = total(2).astype(BF16)
        keep, go = total(1), total(3)

        @pl.when(k == 0)
        def _():
            send(SA.at[k, 1], RA.at[j, 1], s_ra.at[j], r_ra.at[j, 1], along_a[1])
            SA[k, 2] = go.astype(BF16)
            send(SA.at[k, 2], RA.at[j, 0], s_ra.at[j], r_ra.at[j, 0], along_a[3])
            FIN[1] = keep

        @pl.when(k == 1)
        def _():
            send(SA.at[k, 1], RA.at[j, 1], s_ra.at[j], r_ra.at[j, 1], along_a[3])
            SA[k, 0] = keep.astype(BF16)
            send(SA.at[k, 0], RA.at[j, 2], s_ra.at[j], r_ra.at[j, 2], along_a[1])
            FIN[1] = go

    def relay_a(j):
        k = j % 2
        arrived(RA.at[j, 1], r_ra.at[j, 1])

        @pl.when(k == 0)
        def _():
            SA[k, 0] = (FIN[1] + RA[j, 1].astype(F32)).astype(BF16)
            send(SA.at[k, 0], RA.at[j, 2], s_ra.at[j], r_ra.at[j, 2], along_a[1])

        @pl.when(k == 1)
        def _():
            SA[k, 2] = (FIN[1] + RA[j, 1].astype(F32)).astype(BF16)
            send(SA.at[k, 2], RA.at[j, 0], s_ra.at[j], r_ra.at[j, 0], along_a[3])

    def finish_a(j):
        total = KA[j % 2]
        for o in (1, 3):
            arrived(RA.at[j, o - 1], r_ra.at[j, o - 1])
            total += RA[j, o - 1].astype(F32)
        return total

    def finish_x(j):
        o = away(target(j))
        SX[o - 1] = finish_a(j).astype(BF16)
        send(SX.at[o - 1], RX.at[3 - o], s_rx.at[0], r_rx.at[3 - o], device(x + o, a, b, core))

    def slot_grad(q):
        k, n = e + (q // 4) * (1 - 2 * e), q % 4
        some = pl.ds((n % 2) * 2, 2)
        slot = q % 2

        @pl.when(q >= 2)
        def _():
            sent_sg(slot)

        def half_rows(i):
            m = rows_at(i * 320, 320, 64)
            near, far = (W[h, k, n // 2, some].reshape(896, HALF) for h in (0, 1))
            part = (nt(PG[k, m, :HALF], near) + nt(PG[k, m, HALF:], far)).astype(BF16)
            SG[0, rows_at(slot * CAP + i * 320, 320, 64), :] = part[:, :BLK]
            SG[1, rows_at(slot * CAP + i * 320, 320, 64), :384] = part[:, BLK:]

        loop(0, 2, half_rows)
        rows = rows_at(slot * CAP, CAP, 64)
        for i, (at, width) in enumerate(((0, BLK), (BLK, 384))):
            cols = pl.ds(pl.multiple_of(n * 896 + at, 128), width)
            pltpu.make_async_copy(SG.at[i, rows, :width], sg_out.at[k, :, cols], s_sg.at[slot, i]).start()

    def sent_sg(slot):
        arrived(SG.at[0, :CAP, :], s_sg.at[slot, 0])
        arrived(SG.at[1, :CAP, :384], s_sg.at[slot, 1])

    def slot_grads(first, last):
        loop(first, last, slot_grad)

    def gather_step(j):
        @pl.when(j == 3)
        def _():
            first_sends(0)
            pl.semaphore_signal(credit, inc=1, device_id=sib, device_id_type=MESH)

        relay_b(j)

        @pl.when(j == 0)
        def _():
            loop(2, 4, dispatch)

        @pl.when(j > 0)
        def _():
            whole(j - 1)
            forward(j - 1, 0)

        rest_b(j)

        @pl.when(j < 2)
        def _():
            far_a(j + 2)
            send_b(j + 2)

        @pl.when(j == 0)
        def _():
            dispatch(4)

        @pl.when(j > 0)
        def _():
            forward(j - 1, 1)

        @pl.when(j == 1)
        def _():
            loop(5, NBLK, dispatch)

        @pl.when(j == 2)
        def _():
            load_cot.wait()
            pointwise(e)
            theirs(0)
            pltpu.make_async_copy(ACT, act_out.at[0, rows_at(e * CAP, CAP), :], s_loc.at[1]).start()

        @pl.when(j == 3)
        def _():
            arrived(SB, s_sb.at[0])
            theirs(1)

        far_b(j)

        @pl.when(j == 2)
        def _():
            ours(0)

    loop(0, 4, gather_step)

    def reduce_step(j):
        @pl.when(j == 0)
        def _():
            slot_grads(0, 1)

        relayed_sends(j)

        @pl.when(j < 3)
        def _():
            ours(j + 1)

            @pl.when(j >= 1)
            def _():
                sent_b(j - 1)

            first_sends(j + 1)

        @pl.when(j == 0)
        def _():
            pl.semaphore_signal(credit, inc=1, device_id=sib, device_id_type=MESH)
            whole(3)
            forward(3, 0)
            forward(3, 1)
            arrived(PG.at[1 - e], r_cot.at[0])
            arrived(ACT, s_loc.at[1])
            pointwise(1 - e)
            send(ACT, act_out.at[0, rows_at(e * CAP, CAP), :], s_act.at[0], r_act.at[0], along_x[2])

        @pl.when(j < 2)
        def _():
            arrived(SB, s_sb.at[0])
            pl.semaphore_wait(credit, 1)
            theirs(j + 2)

        @pl.when(j >= 1)
        def _():
            relay_a(j - 1)

        @pl.when(j == 2)
        def _():
            finish_x(0)

        @pl.when(j == 3)
        def _():
            FIN[0] = finish_a(1)

        @pl.when(j >= 1)
        def _():
            slot_grads(2 * j, 2 * j + 2)

        @pl.when(j == 0)
        def _():
            slot_grads(1, 2)

        finish_b(j)

    loop(0, 4, reduce_step)
    sent_sg(0)
    sent_sg(1)

    def early(c):
        for k in (0, 1):
            pltpu.make_async_copy(
                sg_out.at[k, :, block_cols(c)], SG.at[c % 2, k * CAP : (k + 1) * CAP], s_cmb.at[c % 2]
            ).start()

    def combine(c):
        arrived(SG.at[c % 2], s_cmb.at[c % 2])

        @pl.when(c >= 2)
        def _():
            arrived(RSB.at[c % 2, :TOK], s_tok.at[c % 2])

        RSB[c % 2, :TOK] = tn(Q[...], SG[c % 2]).astype(BF16)
        pltpu.make_async_copy(RSB.at[c % 2, :TOK], tok_out.at[:, block_cols(c)], s_tok.at[c % 2]).start()

        @pl.when(c + 2 < EARLY)
        def _():
            early(c + 2)

    early(0)
    early(1)
    finish_x(2)
    combine(0)
    relay_a(3)
    loop(1, EARLY, combine)
    gg = ggs[...].astype(F32).T[:8].astype(BF16)
    row = nn(gg, Q[...])
    gate_out[...] = jnp.concatenate([row[:1, i * 128 : (i + 1) * 128] for i in range(8)], axis=0)
    finish_x(3)
    total = FIN[0]
    for o in (1, 2, 3):
        arrived(RX.at[o - 1], r_rx.at[o - 1])
        total += RX[o - 1].astype(F32)
    FIN[0] = total
    away_rows = rows_at((1 - core) * 56, 56, 8)
    kept_rows = rows_at(core * 56, 56, 8)
    last = copy_to(FIN.at[0, away_rows, :], FIN.at[2, away_rows, :], s_fin.at[0], r_fin.at[0], sib)
    last.start()
    last.wait_send()
    arrived(FIN.at[2, kept_rows, :], r_fin.at[0])
    kept, came = FIN[0, kept_rows, :], FIN[2, kept_rows, :]
    wg_out[0, :, :HALF] = jnp.where(core == 0, kept, came)
    wg_out[0, :, HALF:] = jnp.where(core == 0, came, kept)

    arrived(some_pieces(3), s_x.at[0])
    arrived(SX, s_rx.at[0])
    arrived(cot_hbm.at[0, theirs_rows, :], s_cot.at[0])
    arrived(ACT, s_act.at[0])
    arrived(SB, s_sb.at[0])
    arrived(act_out.at[0, theirs_rows, :], r_act.at[0])
    for i in (0, 1):
        arrived(RSB.at[i, :TOK], s_tok.at[i])

    def drain(j):
        arrived(some_pieces(3), s_a.at[j])
        arrived(W.at[0, 0, 0, pl.ds(0, 3)], s_b.at[j])
        arrived(W.at[0, 0, 0], s_sib.at[j])

        @pl.when(j >= 2)
        def _():
            sent_a(j)
            sent_b(j)

    loop(0, 4, drain)


def combine_kernel(
    owner_ref, gate_ref, sg_hbm, tok_hbm, act_hbm, wg_hbm,
    gate_out, tok_out, act_out, wg_out,
    Q, SG, TB, TV, AV, GV, s_sg, s_tok, s_in, s_out,
):
    def cols(c):
        return pl.ds(pl.multiple_of(c * BLK, BLK), BLK)

    def load(c):
        return [
            pltpu.make_async_copy(
                sg_hbm.at[k, :, cols(c)], SG.at[c % 2, k * CAP : (k + 1) * CAP], s_sg.at[c % 2, k]
            )
            for k in (0, 1)
        ]

    moves = [
        (act_hbm, AV, act_out),
        (tok_hbm, TV, tok_out.at[:, : EARLY * BLK]),
        (wg_hbm, GV, wg_out),
    ]
    moves = [
        (pltpu.make_async_copy(p, v, s_in.at[i]), pltpu.make_async_copy(v, q, s_out.at[i]))
        for i, (p, v, q) in enumerate(moves)
    ]
    for c in (EARLY, EARLY + 1):
        for k in load(c):
            k.start()
    for k, _ in moves:
        k.start()
    one_hot_rows(owner_ref, Q)
    gate_out[...] = gate_ref[...].astype(BF16)

    def combine(c):
        for k in load(c):
            k.wait()

        @pl.when(c >= EARLY + 2)
        def _():
            arrived(TB.at[c % 2], s_tok.at[c % 2])

        TB[c % 2] = tn(Q[...], SG[c % 2]).astype(BF16)
        pltpu.make_async_copy(TB.at[c % 2], tok_out.at[:, cols(c)], s_tok.at[c % 2]).start()

        @pl.when(c + 2 < NBLK)
        def _():
            for k in load(c + 2):
                k.start()

    loop(EARLY, EARLY + 1, combine)
    for k, m in moves:
        k.wait()
        m.start()
    loop(EARLY + 1, NBLK, combine)
    for i in (0, 1):
        arrived(TB.at[i], s_tok.at[i])
    for _, m in moves:
        m.wait()


def body(tokens, assignment, gate, weight, cotangent):
    ANY, VMEM = pl.BlockSpec(memory_space=pl.ANY), pl.BlockSpec(memory_space=pltpu.VMEM)
    DMA = pltpu.SemaphoreType.DMA
    shape = jax.ShapeDtypeStruct
    owner = assignment.reshape(1, TOK)
    act, tok, sg, grad_gate, grad_weight = pl.pallas_call(
        main_kernel,
        out_shape=(
            shape((1, 2 * CAP, F), BF16),
            shape((TOK, EARLY * BLK), BF16),
            shape((2, CAP, D), BF16),
            shape((8, 128), F32),
            shape((1, 56, F), F32),
        ),
        in_specs=[VMEM, VMEM, VMEM, ANY, ANY],
        out_specs=(ANY, ANY, ANY, VMEM, VMEM),
        scratch_shapes=[
            pltpu.VMEM((2, 2, 2, 4, 4, ROWS, HALF), BF16),
            pltpu.VMEM((2 * CAP, D), BF16),
            pltpu.VMEM((2 * CAP, TOK), BF16),
            pltpu.VMEM((CAP, F), F32),
            pltpu.VMEM((2, CAP, F), BF16),
            pltpu.VMEM((CAP, F), BF16),
            pltpu.VMEM((2 * CAP, 128), BF16),
            pltpu.VMEM((2 * CAP, 128), BF16),
            pltpu.VMEM((PLANE, HALF), BF16),
            pltpu.VMEM((2, PLANE, HALF), BF16),
            pltpu.VMEM((PLANE, HALF), F32),
            pltpu.VMEM((2, 3, 4, ROWS, HALF), BF16),
            pltpu.VMEM((4, 2, 4, ROWS, HALF), BF16),
            pltpu.VMEM((4, 4, ROWS, HALF), BF16),
            pltpu.VMEM((2, 4, ROWS, HALF), F32),
            pltpu.VMEM((2, 3, ROWS, HALF), BF16),
            pltpu.VMEM((4, 3, ROWS, HALF), BF16),
            pltpu.VMEM((3, ROWS, HALF), BF16),
            pltpu.VMEM((3, ROWS, HALF), BF16),
            pltpu.VMEM((2, ROWS, HALF), F32),
            pltpu.VMEM((3, ROWS, HALF), F32),
            pltpu.VMEM((2, 2 * CAP, BLK), BF16),
            DMA((2,)), DMA((2,)), DMA((1,)), DMA((1,)), DMA((1,)), DMA((3,)), DMA((4,)), DMA((4, 3)),
            DMA((4,)), DMA((4, 2, 2)), DMA((4, 2)), DMA((4,)), DMA((4,)), DMA((1,)), DMA((1,)),
            DMA((1,)), DMA((2,)), pltpu.SemaphoreType.REGULAR, DMA((4,)), DMA((4, 3)),
            DMA((4,)), DMA((4, 2, 2)), DMA((4, 2)), DMA((1,)), DMA((3,)), DMA((1,)), DMA((1,)), DMA((1,)), DMA((1,)),
            DMA((2, 2)), DMA((2,)), DMA((2,)),
        ],
        compiler_params=pltpu.CompilerParams(collective_id=1, has_side_effects=True, vmem_limit_bytes=62 * 2**20),
        name="gather_and_reduce",
    )(weight, owner, gate.reshape(8, 128), tokens, cotangent)
    grad_gate, grad_tokens, activated, grad_weight = pl.pallas_call(
        combine_kernel,
        out_shape=(
            shape((8, 128), BF16),
            shape((TOK, D), BF16),
            shape((1, 2 * CAP, F), BF16),
            shape((1, 56, F), F32),
        ),
        in_specs=[VMEM, VMEM, ANY, ANY, ANY, ANY],
        out_specs=(VMEM, ANY, ANY, ANY),
        scratch_shapes=[
            pltpu.VMEM((2 * CAP, TOK), BF16),
            pltpu.VMEM((2, 2 * CAP, BLK), BF16),
            pltpu.VMEM((2, TOK, BLK), BF16),
            pltpu.VMEM((TOK, EARLY * BLK), BF16),
            pltpu.VMEM((1, 2 * CAP, F), BF16),
            pltpu.VMEM((1, 56, F), F32),
            DMA((2, 2)), DMA((2,)), DMA((3,)), DMA((3,)),
        ],
        compiler_params=pltpu.CompilerParams(vmem_limit_bytes=60 * 2**20),
        name="combine_tokens",
    )(owner, grad_gate, sg, tok, act, grad_weight)
    return activated, grad_tokens, grad_gate.reshape(TOK), grad_weight


def solution(mesh):
    placed = (
        P(("dp", "expert"), None),
        P(("dp", "expert"), None),
        P(("dp", "expert")),
        P("expert", "dp", None),
        P("expert", "dp", None),
    )
    return jax.shard_map(
        body,
        mesh=mesh,
        in_specs=placed,
        out_specs=(
            P("expert", "dp", None),
            P(("dp", "expert"), None),
            P(("dp", "expert")),
            P("expert", "dp", None),
        ),
        check_vma=False,
    )
```
